128 devices in a mesh: seq: 32 (over x, z, y_hi), stream: 4 (over y_lo, core).
Axes of the slice: x: 4, y: 4 (y_hi: 2, y_lo: 2; y = y_hi * 2 + y_lo), z: 4, core: 2. Of those that a mesh axis runs over, the one named last changes fastest.
Arguments:
- features: bfloat16 [4, 16384, 512], P('stream', 'seq'), may hold values from -6 to 6
- dilated_weight: bfloat16 [3, 512, 1024], replicated, may hold values from -0.1875 to 0.1875
- current_weight: bfloat16 [3, 512, 1024], replicated, may hold values from -0.1875 to 0.1875
- residual_weight: bfloat16 [3, 512, 512], replicated, may hold values from -0.25 to 0.25
- predict: bfloat16 [6144, 512], replicated, may hold values from -0.25 to 0.25
- logit_grads: float32 [4, 12, 11, 16384], P('stream', None, None, 'seq'), may hold values from -1.5 to 1.5
- neg_shard: int32 [12, 10], replicated, may hold values from 1 to 31
- neg_frame: int32 [12, 10], replicated, may hold values from 0 to 511
Outputs:
- input_grad: bfloat16 [4, 16384, 512], P('stream', 'seq')
- dilated_grad: float32 [3, 512, 1024], P(None, 'seq')
- current_grad: float32 [3, 512, 1024], P(None, 'seq')
- residual_grad: float32 [3, 512, 512], P(None, 'seq')
The draws below stay inside these ranges and needn't reach their ends.
Inputs may be any that keep to these rules, and one draw needn't show every extreme that they name: The negative of a frame on shard i comes from shard (i + neg_shard) mod 32, never from shard i itself. `neg_frame`: a frame offset within the source shard, taken modulo 512.
All inputs are finite; a program needn't handle non-finite values.
Results may differ from the reference program's by a relative error of at most 0.035.
Values may be sent and summed in bfloat16 or wider, within the bound.
No kernel may reach another device: no remote copies, remote signals or barrier semaphores. Data moves between devices by JAX's collectives and lax.ppermute only.
A program may use at most 192 MiB of HBM per device.

```python
import jax
import jax.numpy as jnp
from jax import lax

C = 512
K = 12
NEG = 10
LAYER_COUNT = 3
FRAMES_DEV = 512
DILATION_NEAREST = 64
DILATION_MIDDLE = 512
DILATION_FARTHEST = 2048
FRAMES = 16384
STREAMS = 4
N_SEQ = 32


def set_ends(result, rng, smallest, high):
    dims = result.shape
    place = [jax.random.randint(jax.random.fold_in(rng, axis), (), 0, dims[axis]) for axis in range(len(dims))]
    result = result.at[tuple(place)].set(smallest)
    longest = dims.index(max(dims))
    place[longest] = (place[longest] + 1) % dims[longest]
    return result.at[tuple(place)].set(high)


def spiked(result, key, source, target, shards_of, factor):
    owner, partner = [(jnp.arange(result.shape[axis_at]) // (result.shape[axis_at] // shards_of)).reshape([-1 if axis == axis_at else 1 for axis in range(result.ndim)]) for axis_at in (source, target)]
    chosen = jax.random.permutation(key, shards_of)[partner]
    strong = (owner == chosen) | (owner == (partner + shards_of // 2) % shards_of)
    return jnp.where(strong, factor * result, result)


def shard_levels(key, dims, pieces, low, high):
    factor_of = 1.0
    for position, parts in pieces:
        draws = jax.random.uniform(jax.random.fold_in(jax.random.fold_in(key, 6), position), (parts,), jnp.float32, low / len(pieces), high / len(pieces))
        factor_of = factor_of * jnp.repeat(jnp.exp(draws), dims[position] // parts).reshape((-1,) + (1,) * (len(dims) - 1 - position))
    return factor_of


def scatter_about(rng, shape, width, bound, split=(), held_as=jnp.bfloat16):
    result = jax.random.normal(rng, shape, jnp.float32) * width
    if len(split) > 0:
        result = shard_levels(rng, shape, split, -0.22, 0.18) * result
    return jnp.clip(result, min=-bound, max=bound).astype(held_as)


def heavy_noise(stream_key, extent, spread, reach, cuts, heavy, kind=jnp.bfloat16):
    entries = spread * jax.random.normal(stream_key, extent, jnp.float32)
    if cuts:
        entries = entries * shard_levels(stream_key, extent, cuts, -0.22, 0.18)
    return jnp.clip(spiked(entries, jax.random.fold_in(stream_key, 3), *heavy), -reach, reach).astype(kind)


def setup_inputs(seed: int = 0) -> dict:
    seeds = jax.random.split(jax.random.key(seed), 9)
    features = heavy_noise(seeds[0], (STREAMS, FRAMES, C), 1.0, 6.0, ((0, 4), (1, 32)), (1, 2, 32, 2.75))
    dilated_weight = scatter_about(seeds[1], (LAYER_COUNT, C, 2 * C), (2 * C) ** -0.5, 0.1875)
    current_weight = scatter_about(seeds[2], (LAYER_COUNT, C, 2 * C), (2 * C) ** -0.5, 0.1875)
    residual_weight = scatter_about(seeds[3], (LAYER_COUNT, C, C), C ** -0.5, 0.25)
    predict = scatter_about(seeds[4], (K * C, C), C ** -0.5, 0.25)
    logit_grads = scatter_about(seeds[5], (STREAMS, K, NEG + 1, FRAMES), 0.1, 1.5, ((0, 4), (3, 32)), jnp.float32)
    neg_shard = set_ends(jax.random.randint(seeds[6], (K, NEG), 1, N_SEQ), jax.random.fold_in(seeds[6], 1), 1, N_SEQ - 1).astype(jnp.int32)
    neg_frame = set_ends(jax.random.randint(seeds[7], (K, NEG), 0, FRAMES_DEV), jax.random.fold_in(seeds[7], 1), 0, FRAMES_DEV - 1).astype(jnp.int32)
    return dict(features=features, dilated_weight=dilated_weight, current_weight=current_weight, residual_weight=residual_weight, predict=predict, logit_grads=logit_grads, neg_shard=neg_shard, neg_frame=neg_frame)


def flat_rows(a):
    return a.reshape(-1, a.shape[-1])


def product(a, b):
    out = jnp.dot(flat_rows(a), b, preferred_element_type=jnp.float32)
    return out.reshape(a.shape[:-1] + (b.shape[-1],))


def product_back(a, b):
    out = lax.dot_general(flat_rows(a), b, (((1,), (1,)), ((), ())), preferred_element_type=jnp.float32)
    return out.reshape(a.shape[:-1] + (b.shape[0],))


def outer_product_sum(a, b):
    return lax.dot_general(flat_rows(a), flat_rows(b), (((0,), (0,)), ((), ())), preferred_element_type=jnp.float32)


def shift_backward(layer_input, dilation_value):
    return jnp.pad(layer_input, ((0, 0), (dilation_value, 0), (0, 0)))[:, :layer_input.shape[1], :]


def shift_forward(layer_input, dilation_value):
    return jnp.pad(layer_input, ((0, 0), (0, dilation_value), (0, 0)))[:, dilation_value:, :]


def reference(features, dilated_weight, current_weight, residual_weight, predict, logit_grads, neg_shard, neg_frame):
    dilation_list = [DILATION_NEAREST, DILATION_MIDDLE, DILATION_FARTHEST]
    chan = features.shape[2]
    layer_input = features
    saved = []
    for layer_index in range(LAYER_COUNT):
        later_rows = shift_backward(layer_input, dilation_list[layer_index])
        pre = product(later_rows, dilated_weight[layer_index]) + product(layer_input, current_weight[layer_index])
        filt = jnp.tanh(pre[..., :chan])
        gate = jax.nn.sigmoid(pre[..., chan:])
        hidden = (filt * gate).astype(jnp.bfloat16)
        saved.append((layer_input, later_rows, filt, gate, hidden))
        layer_input = (layer_input.astype(jnp.float32) + product(hidden, residual_weight[layer_index])).astype(jnp.bfloat16)

    frame = jnp.arange(FRAMES, dtype=jnp.int32)
    shard = frame // FRAMES_DEV
    within = frame % FRAMES_DEV
    total = jnp.zeros(features.shape, jnp.float32)
    for step in range(K):
        positive = shift_forward(features, step + 1)
        mixed = logit_grads[:, step, 0, :, None] * positive.astype(jnp.float32)
        for other in range(NEG):
            source = ((shard + neg_shard[step, other]) % N_SEQ) * FRAMES_DEV + (within + neg_frame[step, other]) % FRAMES_DEV
            picked = jnp.take(features, source.astype(jnp.int32), axis=1)
            mixed = mixed + logit_grads[:, step, other + 1, :, None] * picked.astype(jnp.float32)
        mixed = mixed.astype(jnp.bfloat16)
        total = total + product(mixed, predict[step * chan:(step + 1) * chan])
    gradient_fn = total.astype(jnp.bfloat16)

    dilated_gradients = [None] * LAYER_COUNT
    current_gradients = [None] * LAYER_COUNT
    residual_gradients = [None] * LAYER_COUNT
    for layer_index in reversed(range(LAYER_COUNT)):
        x_in, later_rows, filt, gate, hidden = saved[layer_index]
        dhid = product_back(gradient_fn, residual_weight[layer_index])
        residual_gradients[layer_index] = outer_product_sum(hidden, gradient_fn)
        dfilt = dhid * gate * (1.0 - filt * filt)
        dgate = dhid * filt * gate * (1.0 - gate)
        preactivation_grad = jnp.concatenate([dfilt, dgate], axis=-1).astype(jnp.bfloat16)
        dilated_gradients[layer_index] = outer_product_sum(later_rows, preactivation_grad)
        current_gradients[layer_index] = outer_product_sum(x_in, preactivation_grad)
        local = product_back(preactivation_grad, current_weight[layer_index])
        sent = product_back(preactivation_grad, dilated_weight[layer_index]).astype(jnp.bfloat16)
        gradient_fn = (gradient_fn.astype(jnp.float32) + local + shift_forward(sent, dilation_list[layer_index]).astype(jnp.float32)).astype(jnp.bfloat16)
    return gradient_fn, jnp.stack(dilated_gradients), jnp.stack(current_gradients), jnp.stack(residual_gradients)
```

```python
import functools

import jax
import jax.numpy as jnp
from jax import lax
from jax.experimental import pallas as pl
from jax.experimental.pallas import tpu as pltpu
from jax.sharding import Mesh, PartitionSpec as P

SEQ = ("x", "z", "h")
BF = jnp.bfloat16
F32 = jnp.float32


def rotated(value, axis, steps):
    count = lax.axis_size(axis)
    return lax.ppermute(value, axis, [(i, (i + steps) % count) for i in range(count)])


def shifted(value, steps):
    count = 32
    lead, last = (max(0, -steps), min(count, count - steps))
    return lax.ppermute(value, SEQ, [(i, i + steps) for i in range(lead, last)])


def dot(a, b, ca, cb):
    return lax.dot_general(a, b, (((ca,), (cb,)), ((), ())), preferred_element_type=F32)


def mix_kernel(steps, others, slot, start, own, src_a, src_b, w_a, w_b, p_a, p_b, out_a, out_b, ext, mixed):
    rows = src_a.shape[2]
    half = rows // 2
    for part, (src, w, p, out) in enumerate(((src_a, w_a, p_a, out_a), (src_b, w_b, p_b, out_b))):
        ext[part, 0:4] = src[own[part * 3]]
        after = src[own[part * 3 + 1], 0]
        ext[part, 4] = jnp.where(own[part * 3 + 2] > 0, after, jnp.zeros_like(after))

        def step_body(k, carry, part=part, src=src, w=w):
            lane = lax.broadcasted_iota(jnp.int32, (half, 128), 1)
            for r in range(2):
                at = pl.ds(r * half, half)
                acc = [None] * 4

                def add(j, tiles, f, acc=acc):
                    turned = [pltpu.roll(t, lax.rem(128 - f, 128), 1) for t in tiles]
                    keep = lane < 128 - f
                    for q in range(4):
                        picked = jnp.where(keep, turned[q], turned[(q + 1) % len(tiles)])
                        weight = jnp.broadcast_to(w[k, j : j + 1, q * 128 : (q + 1) * 128], (half, 128))
                        term = picked.astype(F32) * weight
                        acc[q] = term if acc[q] is None else acc[q] + term

                add(0, [ext[part, q, at, :] for q in range(5)], k + 1)
                for j in range(others):
                    n = k * others + j
                    s, at0 = slot[part * steps * others + n], start[n]
                    q0 = lax.shift_right_logical(at0, 7)
                    tiles = [src[s, (q0 + q) & 3, at, :] for q in range(4)]
                    add(j + 1, tiles, at0 & 127)
                for q in range(4):
                    mixed[part, pl.ds(pl.multiple_of(k * rows + r * half, half), half), q * 128 : (q + 1) * 128] = acc[q].astype(BF)
            return carry

        lax.fori_loop(0, steps, step_body, 0)
        out[...] = jnp.dot(p[...], mixed[part], preferred_element_type=F32).astype(BF)


def mix(slot, start, own, src_a, src_b, w_a, w_b, p_a, p_b):
    steps, frames = w_a.shape[0], w_a.shape[2]
    others = w_a.shape[1] - 1
    chan, depth = p_a.shape
    rows = src_a.shape[2]
    smem = pl.BlockSpec(memory_space=pltpu.SMEM)
    vmem = pl.BlockSpec(memory_space=pltpu.VMEM)
    return pl.pallas_call(
        functools.partial(mix_kernel, steps, others),
        out_shape=[jax.ShapeDtypeStruct((chan, frames), BF)] * 2,
        in_specs=[smem] * 3 + [vmem] * 6,
        out_specs=[vmem] * 2,
        scratch_shapes=[
            pltpu.VMEM((2, 5, rows, 128), BF),
            pltpu.VMEM((2, depth, frames), BF),
        ],
        compiler_params=pltpu.CompilerParams(vmem_limit_bytes=40 * 2**20),
        cost_estimate=pl.CostEstimate(flops=12_000_000_000, bytes_accessed=8_000_000, transcendentals=0),
    )(slot, start, own, src_a, src_b, w_a, w_b, p_a, p_b)


def on_device(features, dilated_weight, current_weight, residual_weight, predict, logit_grads, neg_shard, neg_frame):
    _, frames, chan = features.shape
    layers = dilated_weight.shape[0]
    steps, others = neg_shard.shape
    ix, iz, ih = (lax.axis_index(a) for a in SEQ)
    me = (ix * 4 + iz) * 2 + ih
    part_chan = chan // 8

    tiles = features[0].reshape(frames // 128, 128, 8, part_chan).transpose(2, 0, 3, 1)
    block_a = lax.all_to_all(tiles[:4], "x", 0, 0)
    block_b = lax.all_to_all(tiles[4:], "z", 0, 0)
    swap_a, swap_b = rotated(block_a, "h", 1), rotated(block_b, "h", 1)
    logits = logit_grads[0].astype(BF)

    def ring(block, swapped, axis):
        pieces = []
        for d in range(4):
            for v in (block, swapped):
                pieces.append(v if d == 0 else rotated(v, axis, -d))
        return jnp.concatenate(pieces, axis=0)

    src_a = ring(block_a, swap_a, "z")
    src_b = ring(block_b, swap_b, "x")

    def slot_of(shard):
        sx, sz, sh = shard >> 3, (shard >> 1) & 3, shard & 1
        turn = (sh - ih) & 1
        return (((sz - iz) & 3) * 2 + turn) * 4 + sx, (((sx - ix) & 3) * 2 + turn) * 4 + sz

    step_rows = predict.reshape(steps, chan, chan)

    def step_block(at):
        return lax.dynamic_slice_in_dim(step_rows, at, part_chan, axis=1).reshape(steps * part_chan, chan).T

    p_a = step_block(ix * part_chan)
    p_b = step_block((4 + iz) * part_chan)
    start = neg_frame.reshape(-1)
    total = None
    for d in (2, 1, 3, 0):
        target_a = (((ix + d) & 3) * 4 + iz) * 2 + ih
        target_b = (ix * 4 + ((iz + d) & 3)) * 2 + ih
        from_a = slot_of((target_a + neg_shard.reshape(-1)) & 31)[0]
        from_b = slot_of((target_b + neg_shard.reshape(-1)) & 31)[1]
        own = jnp.stack(
            [
                slot_of(target_a)[0],
                slot_of((target_a + 1) & 31)[0],
                (target_a < 31).astype(jnp.int32),
                slot_of(target_b)[1],
                slot_of((target_b + 1) & 31)[1],
                (target_b < 31).astype(jnp.int32),
            ]
        )
        w_a = (logits if d == 0 else rotated(logits, "x", -d)).astype(F32)
        w_b = (logits if d == 0 else rotated(logits, "z", -d)).astype(F32)
        back_a, back_b = mix(jnp.concatenate([from_a, from_b]), start, own, src_a, src_b, w_a, w_b, p_a, p_b)
        if d > 0:
            back_a, back_b = rotated(back_a, "x", d), rotated(back_b, "z", d)
        term = back_a.astype(F32) + back_b.astype(F32)
        total = term if total is None else total + term
    grad = total.astype(BF)

    spans = [(64, 1), (512, 1), (512, 4)]
    layer_in = features[0].T
    saved = []
    for n in range(layers):
        span, hops = spans[n]
        received = shifted(layer_in[:, frames - span :], hops)
        late = received if span == frames else jnp.concatenate([received, layer_in[:, : frames - span]], axis=1)
        pre = dot(dilated_weight[n], late, 0, 0) + dot(current_weight[n], layer_in, 0, 0)
        filt, gate = jnp.tanh(pre[:chan]), jax.nn.sigmoid(pre[chan:])
        hidden = (filt * gate).astype(BF)
        saved.append((layer_in, late, filt, gate, hidden))
        if n + 1 < layers:
            layer_in = (layer_in.astype(F32) + dot(residual_weight[n], hidden, 0, 0)).astype(BF)

    ic = lax.axis_index("c")
    shares = [None] * layers
    for n in reversed(range(layers)):
        layer_in, late, filt, gate, hidden = saved[n]
        span, hops = spans[n]
        dhid = dot(residual_weight[n], grad, 1, 0)
        dpre = jnp.concatenate(
            [dhid * gate * (1.0 - filt * filt), dhid * filt * gate * (1.0 - gate)], axis=0
        ).astype(BF)
        sent = dot(dilated_weight[n], dpre, 1, 0).astype(BF)
        received = shifted(sent[:, :span], -hops)
        local = dot(current_weight[n], dpre, 1, 0)
        by_dilated = dot(late, dpre, 1, 1).astype(BF).reshape(32, 16, 4, 2 * chan // 4)
        by_current = dot(layer_in, dpre, 1, 1).astype(BF).reshape(32, 16, 4, 2 * chan // 4)
        by_residual = dot(hidden, grad, 1, 1).astype(BF).reshape(32, 16, 4, chan // 4)
        stacked = jnp.concatenate([by_dilated, by_current, by_residual], axis=3).transpose(2, 0, 1, 3)
        stacked = stacked.reshape(2, 64, 16, 5 * chan // 4)
        mine = lax.dynamic_index_in_dim(stacked, ic, 0, keepdims=False)
        other = lax.dynamic_index_in_dim(stacked, 1 - ic, 0, keepdims=False)
        both = (mine.astype(F32) + rotated(other, "c", 1).astype(F32)).astype(BF)
        parts = lax.all_to_all(both, ("l",) + SEQ, 0, 0)
        shares[n] = jnp.sum(parts.astype(F32), axis=0).astype(BF)
        if span < frames:
            moved = jnp.concatenate([sent[:, span:], received], axis=1)
        else:
            moved = received
        grad = (grad.astype(F32) + local + moved.astype(F32)).astype(BF)

    whole = lax.all_gather(jnp.stack(shares), ("c", "l")).astype(F32).transpose(1, 2, 0, 3)
    wide = 2 * chan // 4
    return (
        grad.T[None],
        whole[..., :wide].reshape(layers, 16, 2 * chan),
        whole[..., wide : 2 * wide].reshape(layers, 16, 2 * chan),
        whole[..., 2 * wide :].reshape(layers, 16, chan),
    )


def solution(mesh):
    fine = Mesh(mesh.devices.reshape(4, 4, 2, 2, 2), ("x", "z", "h", "l", "c"))
    stream = ("l", "c")
    return jax.shard_map(
        on_device,
        mesh=fine,
        in_specs=(P(stream, SEQ, None), P(), P(), P(), P(), P(stream, None, None, SEQ), P(), P()),
        out_specs=(P(stream, SEQ, None), P(None, SEQ, None), P(None, SEQ, None), P(None, SEQ, None)),
        check_vma=False,
    )
```

```python
import functools

import jax
import jax.numpy as jnp
from jax import lax
from jax.experimental import pallas as pl
from jax.experimental.pallas import tpu as pltpu
from jax.sharding import Mesh, PartitionSpec as P

SEQ = ("x", "z", "h")
BF = jnp.bfloat16
F32 = jnp.float32


def rotated(value, axis, steps):
    count = lax.axis_size(axis)
    return lax.ppermute(value, axis, [(i, (i + steps) % count) for i in range(count)])


def shifted(value, steps):
    count = 32
    lead, last = (max(0, -steps), min(count, count - steps))
    return lax.ppermute(value, SEQ, [(i, i + steps) for i in range(lead, last)])


def dot(a, b, ca, cb):
    return lax.dot_general(a, b, (((ca,), (cb,)), ((), ())), preferred_element_type=F32)


def mix_kernel(steps, others, slot, start, own, src_a, src_b, w_a, w_b, p_a, p_b, out_a, out_b, ext, mixed):
    rows = src_a.shape[2]
    half = rows // 2
    for part, (src, w, p, out) in enumerate(((src_a, w_a, p_a, out_a), (src_b, w_b, p_b, out_b))):
        ext[part, 0:4] = src[own[part * 3]]
        after = src[own[part * 3 + 1], 0]
        ext[part, 4] = jnp.where(own[part * 3 + 2] > 0, after, jnp.zeros_like(after))

        def step_body(k, carry, part=part, src=src, w=w):
            lane = lax.broadcasted_iota(jnp.int32, (half, 128), 1)
            for r in range(2):
                at = pl.ds(r * half, half)
                acc = [None] * 4

                def add(j, tiles, f, acc=acc):
                    turned = [pltpu.roll(t, lax.rem(128 - f, 128), 1) for t in tiles]
                    keep = lane < 128 - f
                    for q in range(4):
                        picked = jnp.where(keep, turned[q], turned[(q + 1) % len(tiles)])
                        weight = jnp.broadcast_to(w[k, j : j + 1, q * 128 : (q + 1) * 128], (half, 128))
                        term = picked.astype(F32) * weight
                        acc[q] = term if acc[q] is None else acc[q] + term

                add(0, [ext[part, q, at, :] for q in range(5)], k + 1)
                for j in range(others):
                    n = k * others + j
                    s, at0 = slot[part * steps * others + n], start[n]
                    q0 = lax.shift_right_logical(at0, 7)
                    tiles = [src[s, (q0 + q) & 3, at, :] for q in range(4)]
                    add(j + 1, tiles, at0 & 127)
                for q in range(4):
                    mixed[part, pl.ds(pl.multiple_of(k * rows + r * half, half), half), q * 128 : (q + 1) * 128] = acc[q].astype(BF)
            return carry

        lax.fori_loop(0, steps, step_body, 0)
        out[...] = jnp.dot(p[...], mixed[part], preferred_element_type=F32).astype(BF)


def mix(slot, start, own, src_a, src_b, w_a, w_b, p_a, p_b):
    steps, frames = w_a.shape[0], w_a.shape[2]
    others = w_a.shape[1] - 1
    chan, depth = p_a.shape
    rows = src_a.shape[2]
    smem = pl.BlockSpec(memory_space=pltpu.SMEM)
    vmem = pl.BlockSpec(memory_space=pltpu.VMEM)
    return pl.pallas_call(
        functools.partial(mix_kernel, steps, others),
        out_shape=[jax.ShapeDtypeStruct((chan, frames), BF)] * 2,
        in_specs=[smem] * 3 + [vmem] * 6,
        out_specs=[vmem] * 2,
        scratch_shapes=[
            pltpu.VMEM((2, 5, rows, 128), BF),
            pltpu.VMEM((2, depth, frames), BF),
        ],
        compiler_params=pltpu.CompilerParams(vmem_limit_bytes=40 * 2**20),
        cost_estimate=pl.CostEstimate(flops=12_000_000_000, bytes_accessed=8_000_000, transcendentals=0),
    )(slot, start, own, src_a, src_b, w_a, w_b, p_a, p_b)


def forward_kernel(late, x, by_late, by_x, by_hidden, hidden, slope_f, slope_g, *after):
    chan = x.shape[0]
    pre_f = dot(by_late[:, :chan], late[...], 0, 0) + dot(by_x[:, :chan], x[...], 0, 0)
    filt = jnp.tanh(pre_f)
    pre_g = dot(by_late[:, chan:], late[...], 0, 0) + dot(by_x[:, chan:], x[...], 0, 0)
    gate = 0.5 * jnp.tanh(0.5 * pre_g) + 0.5
    out = filt * gate
    hidden[...] = out.astype(BF)
    slope_f[...] = (gate * (1.0 - filt * filt)).astype(BF)
    slope_g[...] = (out * (1.0 - gate)).astype(BF)
    if after:
        after[0][...] = (x[...].astype(F32) + dot(by_hidden[...], hidden[...], 0, 0)).astype(BF)


def kernel_call(body, outs, ins, flops, scratch=(), smem=0, limit=24):
    vmem = pl.BlockSpec(memory_space=pltpu.VMEM)
    size = sum(v.size * v.dtype.itemsize for v in ins) + sum(v.size * v.dtype.itemsize for v in outs)
    return pl.pallas_call(
        body,
        out_shape=outs,
        in_specs=[pl.BlockSpec(memory_space=pltpu.SMEM)] * smem + [vmem] * (len(ins) - smem),
        out_specs=[vmem] * len(outs),
        scratch_shapes=list(scratch),
        compiler_params=pltpu.CompilerParams(vmem_limit_bytes=limit * 2**20),
        cost_estimate=pl.CostEstimate(flops=flops, bytes_accessed=size, transcendentals=0),
    )(*ins)


def forward(late, x, by_late, by_x, by_hidden, last):
    shape = jax.ShapeDtypeStruct(x.shape, BF)
    return kernel_call(forward_kernel, [shape] * (3 if last else 4), [late, x, by_late, by_x, by_hidden], 1_342_177_280)


def first_kernel(count, *refs):
    terms, (by_hidden, by_late, slope_f, slope_g, grad, dpre, sent) = refs[:count], refs[count:]
    chan = grad.shape[0]
    total = terms[0][...].astype(F32)
    for term in terms[1:]:
        total = total + term[...].astype(F32)
    grad[...] = total.astype(BF)
    dhid = jnp.dot(by_hidden[...], grad[...], preferred_element_type=F32)
    dpre[:chan] = (dhid * slope_f[...].astype(F32)).astype(BF)
    dpre[chan:] = (dhid * slope_g[...].astype(F32)).astype(BF)
    sent[...] = jnp.dot(by_late[...], dpre[...], preferred_element_type=F32).astype(BF)


def first(terms, by_hidden, by_late, slope_f, slope_g):
    chan, frames = slope_f.shape
    outs = [jax.ShapeDtypeStruct((n, frames), BF) for n in (chan, 2 * chan, chan)]
    ins = list(terms) + [by_hidden, by_late, slope_f, slope_g]
    return kernel_call(functools.partial(first_kernel, len(terms)), outs, ins, 805_306_368)


def rest_kernel(core, grad, dpre, late, x, hidden, by_x, part, mine, other):
    chan = x.shape[0]
    part[...] = grad[...].astype(F32) + jnp.dot(by_x[...], dpre[...], preferred_element_type=F32)
    for out, at in ((other, 1 - core[0]), (mine, core[0])):
        rows = dpre[pl.ds(pl.multiple_of(at * chan, chan), chan), :]
        out[:, :chan] = dot(late[...], rows, 1, 1).astype(BF)
        out[:, chan : 2 * chan] = dot(x[...], rows, 1, 1).astype(BF)
        rows = grad[pl.ds(pl.multiple_of(at * (chan // 2), chan // 2), chan // 2), :]
        out[:, 2 * chan :] = dot(hidden[...], rows, 1, 1).astype(BF)


def rest(core, grad, dpre, late, x, hidden, by_x):
    chan, frames = x.shape
    outs = [jax.ShapeDtypeStruct((chan, frames), F32)] + [jax.ShapeDtypeStruct((chan, 5 * chan // 2), BF)] * 2
    return kernel_call(rest_kernel, outs, [core, grad, dpre, late, x, hidden, by_x], 1_879_048_192, smem=1)


def on_device(features, dilated_weight, current_weight, residual_weight, predict, logit_grads, neg_shard, neg_frame):
    _, frames, chan = features.shape
    layers = dilated_weight.shape[0]
    steps, others = neg_shard.shape
    ix, iz, ih = (lax.axis_index(a) for a in SEQ)
    me = (ix * 4 + iz) * 2 + ih
    part_chan = chan // 8

    tiles = features[0].reshape(frames // 128, 128, 8, part_chan).transpose(2, 0, 3, 1)
    block_a = lax.all_to_all(tiles[:4], "x", 0, 0)
    block_b = lax.all_to_all(tiles[4:], "z", 0, 0)
    swap_a, swap_b = rotated(block_a, "h", 1), rotated(block_b, "h", 1)
    logits = logit_grads[0].astype(BF)

    def ring(block, swapped, axis):
        pieces = []
        for d in range(4):
            for v in (block, swapped):
                pieces.append(v if d == 0 else rotated(v, axis, -d))
        return jnp.concatenate(pieces, axis=0)

    src_a = ring(block_a, swap_a, "z")
    src_b = ring(block_b, swap_b, "x")

    def slot_of(shard):
        sx, sz, sh = shard >> 3, (shard >> 1) & 3, shard & 1
        turn = (sh - ih) & 1
        return (((sz - iz) & 3) * 2 + turn) * 4 + sx, (((sx - ix) & 3) * 2 + turn) * 4 + sz

    step_rows = predict.reshape(steps, chan, chan)

    def step_block(at):
        return lax.dynamic_slice_in_dim(step_rows, at, part_chan, axis=1).reshape(steps * part_chan, chan).T

    p_a = step_block(ix * part_chan)
    p_b = step_block((4 + iz) * part_chan)
    start = neg_frame.reshape(-1)
    terms = []
    for d in (2, 1, 3, 0):
        target_a = (((ix + d) & 3) * 4 + iz) * 2 + ih
        target_b = (ix * 4 + ((iz + d) & 3)) * 2 + ih
        from_a = slot_of((target_a + neg_shard.reshape(-1)) & 31)[0]
        from_b = slot_of((target_b + neg_shard.reshape(-1)) & 31)[1]
        own = jnp.stack(
            [
                slot_of(target_a)[0],
                slot_of((target_a + 1) & 31)[0],
                (target_a < 31).astype(jnp.int32),
                slot_of(target_b)[1],
                slot_of((target_b + 1) & 31)[1],
                (target_b < 31).astype(jnp.int32),
            ]
        )
        w_a = (logits if d == 0 else rotated(logits, "x", -d)).astype(F32)
        w_b = (logits if d == 0 else rotated(logits, "z", -d)).astype(F32)
        back_a, back_b = mix(jnp.concatenate([from_a, from_b]), start, own, src_a, src_b, w_a, w_b, p_a, p_b)
        if d > 0:
            back_a, back_b = rotated(back_a, "x", d), rotated(back_b, "z", d)
        terms += [back_a, back_b]

    spans = [(64, 1), (512, 1), (512, 4)]
    layer_in = features[0].T
    saved = []
    for n in range(layers):
        span, hops = spans[n]
        received = shifted(layer_in[:, frames - span :], hops)
        late = received if span == frames else jnp.concatenate([received, layer_in[:, : frames - span]], axis=1)
        out = forward(late, layer_in, dilated_weight[n], current_weight[n], residual_weight[n], n + 1 == layers)
        saved.append((layer_in, late) + tuple(out[:3]))
        layer_in = out[-1]

    core = lax.axis_index("c")
    shares = [None] * layers
    for n in reversed(range(layers)):
        layer_in, late, hidden, slope_f, slope_g = saved[n]
        span, hops = spans[n]
        grad, dpre, sent = first(terms, residual_weight[n], dilated_weight[n], slope_f, slope_g)
        received = shifted(sent[:, :span], -hops)
        part, mine, other = rest(core[None], grad, dpre, late, layer_in, hidden, current_weight[n])
        both = (mine.astype(F32) + rotated(other, "c", 1).astype(F32)).astype(BF)
        parts = lax.all_to_all(both.reshape(32, 16, 5 * chan // 2), SEQ, 0, 0)
        shares[n] = jnp.sum(parts.astype(F32), axis=0).astype(BF)
        if span < frames:
            received = jnp.concatenate([sent[:, span:], received], axis=1)
        terms = [part, received]
    grad = (terms[0] + terms[1].astype(F32)).astype(BF)

    share = jnp.stack(shares)
    share = share.astype(F32) + rotated(share, "l", 1).astype(F32)
    far = rotated(share, "c", 1)
    low, high = jnp.where(core == 0, share, far), jnp.where(core == 0, far, share)

    def columns(at, size):
        return jnp.concatenate([low[..., at : at + size], high[..., at : at + size]], axis=-1)

    return (
        grad.T[None],
        columns(0, chan),
        columns(chan, chan),
        columns(2 * chan, chan // 2),
    )


def solution(mesh):
    fine = Mesh(mesh.devices.reshape(4, 4, 2, 2, 2), ("x", "z", "h", "l", "c"))
    stream = ("l", "c")
    return jax.shard_map(
        on_device,
        mesh=fine,
        in_specs=(P(stream, SEQ, None), P(), P(), P(), P(), P(stream, None, None, SEQ), P(), P()),
        out_specs=(P(stream, SEQ, None), P(None, SEQ, None), P(None, SEQ, None), P(None, SEQ, None)),
        check_vma=False,
    )
```

```python
import functools

import jax
import jax.numpy as jnp
from jax import lax
from jax.experimental import pallas as pl
from jax.experimental.pallas import tpu as pltpu
from jax.sharding import Mesh, PartitionSpec as P

SEQ = ("x", "z", "h")
BF = jnp.bfloat16
F32 = jnp.float32
VMEM = pl.BlockSpec(memory_space=pltpu.VMEM)
SMEM = pl.BlockSpec(memory_space=pltpu.SMEM)
ANY = pl.BlockSpec(memory_space=pl.ANY)
PACE = 1e9


def rotated(value, axis, steps):
    count = lax.axis_size(axis)
    return lax.ppermute(value, axis, [(i, (i + steps) % count) for i in range(count)])


def shifted(value, steps):
    count = 32
    lead, last = (max(0, -steps), min(count, count - steps))
    return lax.ppermute(value, SEQ, [(i, i + steps) for i in range(lead, last)])


def dot(a, b, ca, cb):
    return lax.dot_general(a, b, (((ca,), (cb,)), ((), ())), preferred_element_type=F32)


def like(*shape, dtype=BF):
    return jax.ShapeDtypeStruct(shape, dtype)


def held_for(*weights):
    return [pltpu.VMEM(w.shape[1:], w.dtype) for w in weights] + [pltpu.SemaphoreType.DMA((len(weights),))]


def fetched(n, stacks, held, sems):
    copies = [pltpu.make_async_copy(w.at[n], h, sems.at[m]) for m, (w, h) in enumerate(zip(stacks, held))]
    for copy in copies:
        copy.start()
    return copies


def kernel_call(body, outs, ins, specs=None, scratch=(), limit=12, cost=2.0):
    return pl.pallas_call(
        body,
        out_shape=outs,
        in_specs=specs or [VMEM] * len(ins),
        out_specs=[VMEM] * len(outs),
        scratch_shapes=list(scratch),
        compiler_params=pltpu.CompilerParams(vmem_limit_bytes=limit * 2**20),
        cost_estimate=pl.CostEstimate(flops=int(cost * PACE) + 1, bytes_accessed=1, transcendentals=0),
    )(*ins)


def prepare_kernel(place, features, turned, *blocks):
    frames, rows = turned.shape[1], blocks[0].shape[1]
    for q in range(frames // 128):
        turned[:, q * 128 : (q + 1) * 128] = features[0, q * 128 : (q + 1) * 128, :].T
    for n, block in enumerate(blocks):
        at = pl.multiple_of((n // 4 * 4 + ((place[n // 4] + n % 4) & 3)) * rows, rows)
        for q in range(frames // 128):
            block[q] = turned[pl.ds(at, rows), q * 128 : (q + 1) * 128]


def prepare(place, features):
    _, frames, chan = features.shape
    outs = [like(chan, frames)] + [like(frames // 128, chan // 8, 128)] * 8
    turned, *blocks = kernel_call(prepare_kernel, outs, [place, features], [SMEM, VMEM])
    return turned, blocks[:4], blocks[4:]


def pack_kernel(*refs):
    blocks, logits, outs = (refs[:4], refs[4:8]), refs[8], refs[9:]
    steps, width = logits.shape[1:3]
    tiles = blocks[0][0].shape[0]
    for part in range(2):
        pack, sole = outs[part], outs[2 + part]
        for n, block in enumerate(blocks[part]):
            pack[n * tiles : (n + 1) * tiles] = block[...]
            sole[n * tiles : (n + 1) * tiles] = block[...]
        for q in range(tiles):
            for k in range(steps):
                n = q * steps + k
                value = logits[0, k, :, q * 128 : (q + 1) * 128].astype(BF)
                pack[4 * tiles + n // 4, n % 4 * 16 : n % 4 * 16 + width, :] = value
                rest = jnp.zeros((16 - width, 128), BF)
                pack[4 * tiles + n // 4, n % 4 * 16 + width : n % 4 * 16 + 16, :] = rest


def pack(blocks_a, blocks_b, logits):
    tiles, rows, _ = blocks_a[0].shape
    steps = logits.shape[1]
    outs = [like(4 * tiles + tiles * steps // 4, rows, 128)] * 2 + [like(4 * tiles, rows, 128)] * 2
    return kernel_call(pack_kernel, outs, [*blocks_a, *blocks_b, logits])


def predict_kernel(place, predict, out_a, out_b, rows, sems):
    steps = sems.shape[1]
    chan = predict.shape[1]
    size = rows.shape[1] // steps
    copies = []
    for part, at in enumerate((place[0], 4 + place[1])):
        for k in range(steps):
            copies.append(
                pltpu.make_async_copy(
                    predict.at[pl.ds(pl.multiple_of(k * chan + at * size, size), size), :],
                    rows.at[part, pl.ds(k * size, size), :],
                    sems.at[part, k],
                )
            )
    for copy in copies:
        copy.start()
    for copy in copies:
        copy.wait()
    out_a[...] = rows[0].T
    out_b[...] = rows[1].T


def mix_kernel(jobs, steps, others, shard, frame, place, *refs):
    parts = sorted({part for job in jobs for part, _ in job})
    order = [pair for job in jobs for pair in job]
    refs = list(refs)
    pieces = {part: [refs.pop(0) for _ in range(8)] for part in parts}
    rows_of = {part: refs.pop(0) for part in parts}
    packs = [refs.pop(0) for _ in order]
    outs = [refs.pop(0) for _ in jobs]
    src, ext, packed, wide, mixed, sems = refs
    count, rows, _ = pieces[parts[0]][1].shape
    tiles = count // 4
    half = rows // 2
    ix, iz, ih = place[0], place[1], place[2]

    def fetch(n):
        size = packed.shape[1]
        return pltpu.make_async_copy(packs[n].at[pl.ds(count, size)], packed.at[n % 2], sems.at[n % 2])

    fetch(0).start()
    for at, part in enumerate(parts):
        for n, piece in enumerate(pieces[part]):
            src[at, n * count : (n + 1) * count] = piece[:count]

    def slot_of(part, index):
        x, z = index >> 3, (index >> 1) & 3
        far, near = (z - iz, ix - x) if part == 0 else (x - ix, iz - z)
        return (((far & 3) * 2 + ((index - ih) & 1)) * 4 + (near & 3)) * tiles

    turn = 0
    for job, out in zip(jobs, outs):
        total = None
        for part, distance in job:
            fetch(turn).wait()
            if turn + 1 < len(order):
                fetch(turn + 1).start()
            for n in range(wide.shape[0]):
                wide[n] = packed[turn % 2, n // 4, n % 4 * 16 : n % 4 * 16 + 16, :].astype(F32)
            turn += 1
            held = src.at[parts.index(part)]
            x, z = ((ix + distance) & 3, iz) if part == 0 else (ix, (iz + distance) & 3)
            target = (x * 4 + z) * 2 + ih
            ext[0:tiles] = held[pl.ds(slot_of(part, target), tiles)]
            after = held[slot_of(part, (target + 1) & 31)]
            ext[tiles] = jnp.where(target < 31, after, jnp.zeros_like(after))

            def step_body(k, carry, part=part, held=held, target=target):
                lane = lax.broadcasted_iota(jnp.int32, (half, 128), 1)
                found = [(slot_of(part, (target + shard[k, j]) & 31), frame[k, j]) for j in range(others)]
                for r in range(2):
                    at = pl.ds(r * half, half)
                    acc = [None] * tiles

                    def add(j, values, f):
                        turned = [pltpu.roll(t, lax.rem(128 - f, 128), 1) for t in values]
                        keep = lane < 128 - f
                        for q in range(tiles):
                            picked = jnp.where(keep, turned[q], turned[(q + 1) % len(values)])
                            weight = jnp.broadcast_to(wide[q * steps + k, j : j + 1, :], (half, 128))
                            term = picked.astype(F32) * weight
                            acc[q] = term if acc[q] is None else acc[q] + term

                    add(0, [ext[q, at, :] for q in range(tiles + 1)], k + 1)
                    for j, (s, at0) in enumerate(found):
                        q0 = lax.shift_right_logical(at0, 7)
                        add(j + 1, [held[s + ((q0 + q) & (tiles - 1)), at, :] for q in range(tiles)], at0 & 127)
                    for q in range(tiles):
                        mixed[pl.ds(pl.multiple_of(k * rows + r * half, half), half), q * 128 : (q + 1) * 128] = acc[q].astype(BF)
                return carry

            lax.fori_loop(0, steps, step_body, 0, unroll=2)
            term = jnp.dot(rows_of[part][...], mixed[...], preferred_element_type=F32)
            total = term if total is None else total + term
        out[...] = total.astype(BF)


def mix(jobs, shard, frame, place, pieces, rows_of, packs):
    parts = sorted({part for job in jobs for part, _ in job})
    steps, others = shard.shape
    chan, depth = rows_of[0].shape
    count, rows, _ = pieces[0][1].shape
    tiles, held = count // 4, packs[0][0].shape[0] - count
    frames = tiles * 128
    scratch = [
        pltpu.VMEM((len(parts), 8 * count, rows, 128), BF),
        pltpu.VMEM((tiles + 1, rows, 128), BF),
        pltpu.VMEM((2, held, rows, 128), BF),
        pltpu.VMEM((tiles * steps, 16, 128), F32),
        pltpu.VMEM((depth, frames), BF),
        pltpu.SemaphoreType.DMA((2,)),
    ]
    ins = [shard, frame, place] + [v for part in parts for v in pieces[part]] + [rows_of[part] for part in parts]
    last = [packs[part][distance] for job in jobs for part, distance in job]
    body = functools.partial(mix_kernel, jobs, steps, others)
    specs = [SMEM] * 3 + [VMEM] * (len(ins) - 3) + [ANY] * len(last)
    return kernel_call(body, [like(chan, frames)] * len(jobs), ins + last, specs, scratch, limit=16, cost=4.0 * len(last))


def forward_kernel(n, span, last, received, x, *refs):
    stacks, outs, (by_late, by_x, by_hidden, sems) = refs[:3], list(refs[3:-4]), refs[-4:]
    copies = fetched(n, stacks, (by_late, by_x, by_hidden), sems)
    chan, frames = x.shape
    late = received
    if span < frames:
        late = outs.pop(0)
        late[:, :span] = received[...]
        late[:, span:] = x[:, : frames - span]
    hidden, slope_f, slope_g = outs[:3]
    for copy in copies:
        copy.wait()
    filt = jnp.tanh(dot(by_late[:, :chan], late[...], 0, 0) + dot(by_x[:, :chan], x[...], 0, 0))
    pre = dot(by_late[:, chan:], late[...], 0, 0) + dot(by_x[:, chan:], x[...], 0, 0)
    gate = 0.5 * jnp.tanh(0.5 * pre) + 0.5
    out = filt * gate
    hidden[...] = out.astype(BF)
    slope_f[...] = (gate * (1.0 - filt * filt)).astype(BF)
    slope_g[...] = (out * (1.0 - gate)).astype(BF)
    if not last:
        outs[3][...] = (x[...].astype(F32) + dot(by_hidden[...], hidden[...], 0, 0)).astype(BF)


def forward(n, last, span, received, x, by_late, by_x, by_hidden):
    count = (span < x.shape[1]) + 3 + (not last)
    outs = kernel_call(
        functools.partial(forward_kernel, n, span, last),
        [like(*x.shape)] * count,
        [received, x, by_late, by_x, by_hidden],
        [VMEM, VMEM] + [ANY] * 3,
        held_for(by_late, by_x, by_hidden),
        limit=12,
    )
    return outs if span < x.shape[1] else [received] + list(outs)


def first_kernel(n, count, *refs):
    terms, (slope_f, slope_g), stacks = refs[:count], refs[count : count + 2], refs[count + 2 : count + 4]
    grad, dpre, sent, by_hidden, by_late, sems = refs[count + 4 :]
    copies = fetched(n, stacks, (by_hidden, by_late), sems)
    chan = grad.shape[0]
    total = terms[0][...].astype(F32)
    for term in terms[1:]:
        total = total + term[...].astype(F32)
    grad[...] = total.astype(BF)
    copies[0].wait()
    dhid = jnp.dot(by_hidden[...], grad[...], preferred_element_type=F32)
    dpre[:chan] = (dhid * slope_f[...].astype(F32)).astype(BF)
    dpre[chan:] = (dhid * slope_g[...].astype(F32)).astype(BF)
    copies[1].wait()
    sent[...] = jnp.dot(by_late[...], dpre[...], preferred_element_type=F32).astype(BF)


def first(n, terms, by_hidden, by_late, slope_f, slope_g):
    chan, frames = slope_f.shape
    outs = [like(m, frames) for m in (chan, 2 * chan, chan)]
    ins = list(terms) + [slope_f, slope_g, by_hidden, by_late]
    specs = [VMEM] * (len(ins) - 2) + [ANY] * 2
    return kernel_call(functools.partial(first_kernel, n, len(terms)), outs, ins, specs, held_for(by_hidden, by_late))


def rest_kernel(n, place, grad, dpre, late, x, hidden, stack, part, mine, other, by_x, sems):
    chan = x.shape[0]
    copies = fetched(n, (stack,), (by_x,), sems)
    core = place[3]
    for out, at in ((other, 1 - core), (mine, core)):
        rows = dpre[pl.ds(pl.multiple_of(at * chan, chan), chan), :]
        out[:, :chan] = dot(late[...], rows, 1, 1).astype(BF)
        out[:, chan : 2 * chan] = dot(x[...], rows, 1, 1).astype(BF)
        rows = grad[pl.ds(pl.multiple_of(at * (chan // 2), chan // 2), chan // 2), :]
        out[:, 2 * chan :] = dot(hidden[...], rows, 1, 1).astype(BF)
    copies[0].wait()
    part[...] = grad[...].astype(F32) + jnp.dot(by_x[...], dpre[...], preferred_element_type=F32)


def rest(n, place, grad, dpre, late, x, hidden, by_x):
    chan, frames = x.shape
    outs = [like(chan, frames, dtype=F32)] + [like(chan, 5 * chan // 2)] * 2
    specs = [SMEM] + [VMEM] * 5 + [ANY]
    ins = [place, grad, dpre, late, x, hidden, by_x]
    return kernel_call(functools.partial(rest_kernel, n), outs, ins, specs, held_for(by_x))


def pair_kernel(place, *refs):
    values, outs = refs[:-8], refs[-8:]
    count, rows, half = outs[0].shape
    for n in range(count):
        a, b = values[2 * n], values[2 * n + 1]

        def total(at, size, columns):
            span = pl.ds(pl.multiple_of(at, 16), size)
            return (a[span, columns].astype(F32) + b[span, columns].astype(F32)).astype(BF)

        for d in range(4):
            outs[d][n] = total(((place[0] + d) & 3) * rows, rows, slice(0, half))
            size = rows // 4
            for x in range(4):
                outs[4 + d][n, x] = total(x * rows + ((place[1] + d) & 3) * size, size, slice(half, 2 * half))


def pair(place, *values):
    chan, width = values[0].shape
    count, rows, half = len(values) // 2, chan // 4, width // 2
    outs = [like(count, rows, half)] * 4 + [like(count, 4, rows // 4, half)] * 4
    outs = kernel_call(pair_kernel, outs, [place, *values], [SMEM] + [VMEM] * len(values))
    return exchanged(outs, "x", "z")


def exchanged(values, first_axis, second_axis):
    return [
        v if n % 4 == 0 else rotated(v, (first_axis, second_axis)[n // 4], n % 4) for n, v in enumerate(values)
    ]


def middle_kernel(place, *refs):
    groups, outs = (refs[:8], refs[8:16]), refs[16:]
    size = outs[0].shape[1]
    at = 0
    for group in groups:
        for n in range(group[0].shape[0]):
            for d in range(4):
                rows = pl.ds(pl.multiple_of(((place[1] + d) & 3) * size, size), size)
                total = group[0][n, rows, :].astype(F32)
                for m in range(1, 4):
                    total = total + group[m][n, rows, :].astype(F32)
                outs[d][at] = total.astype(BF)
                x = (place[0] + d) & 3
                total = group[4][n, x].astype(F32)
                for m in range(5, 8):
                    total = total + group[m][n, x].astype(F32)
                outs[4 + d][at] = total.astype(BF)
            at += 1


def middle(place, *groups):
    layers = sum(group[0].shape[0] for group in groups)
    _, rows, half = groups[0][0].shape
    ins = [place] + [v for group in groups for v in group]
    outs = kernel_call(middle_kernel, [like(layers, rows // 4, half)] * 8, ins, [SMEM] + [VMEM] * (len(ins) - 1))
    return exchanged(outs, "z", "x")


def late_kernel(place, *refs):
    parts, (keep, away) = refs[:8], refs[8:]
    rows, half = keep.shape[1], parts[0].shape[2]
    for out, h in ((away, 1 - place[2]), (keep, place[2])):
        span = pl.ds(pl.multiple_of(h * rows, rows), rows)
        for side in range(2):
            total = parts[4 * side][:, span, :].astype(F32)
            for m in range(1, 4):
                total = total + parts[4 * side + m][:, span, :].astype(F32)
            out[:, :, side * half : (side + 1) * half] = total.astype(BF)


def streams_kernel(keep, over_h, over_l, over_both, out):
    near = keep[...].astype(F32) + over_h[...].astype(F32)
    out[...] = near + (over_l[...].astype(F32) + over_both[...].astype(F32))


def split_kernel(place, mine, other, *outs):
    core = place[3]
    a, b = mine[...], other[...]
    low, high = jnp.where(core == 0, a, b), jnp.where(core == 0, b, a)
    at = 0
    for out in outs:
        size = out.shape[2] // 2
        out[:, :, :size] = low[:, :, at : at + size]
        out[:, :, size:] = high[:, :, at : at + size]
        at += size


def final_kernel(span, part, sent, received, out):
    chan, frames = part.shape
    total = (part[:, : frames - span] + sent[:, span:].astype(F32)).astype(BF)
    out[0, : frames - span] = total.T
    total = (part[:, frames - span :] + received[...].astype(F32)).astype(BF)
    out[0, frames - span :] = total.T


def on_device(features, dilated_weight, current_weight, residual_weight, predict, logit_grads, neg_shard, neg_frame):
    _, frames, chan = features.shape
    layers = dilated_weight.shape[0]
    steps, others = neg_shard.shape
    rows = chan // 8
    place = jnp.stack([lax.axis_index(a) for a in ("x", "z", "h", "c")])

    turned, blocks_a, blocks_b = prepare(place, features)
    rows_of = kernel_call(
        predict_kernel,
        [like(chan, steps * rows)] * 2,
        [place, predict],
        [SMEM, ANY],
        [pltpu.VMEM((2, steps * rows, chan), BF), pltpu.SemaphoreType.DMA((2, steps))],
        cost=4.0,
    )
    blocks_a = blocks_a[:1] + [rotated(blocks_a[d], "x", d) for d in (1, 2, 3)]
    blocks_b = blocks_b[:1] + [rotated(blocks_b[d], "z", d) for d in (1, 2, 3)]
    blocks_a, rows_of = lax.optimization_barrier((blocks_a, rows_of))
    pack_a, pack_b, sole_a, sole_b = pack(blocks_a, blocks_b, logit_grads)
    sole_a, sole_b = rotated(sole_a, "h", 1), rotated(sole_b, "h", 1)
    packs_a = [pack_a] + [rotated(pack_a, "z", -d) for d in (1, 2, 3)]
    packs_b = [pack_b] + [rotated(pack_b, "x", -d) for d in (1, 2, 3)]
    soles_a = [sole_a] + [rotated(sole_a, "z", -d) for d in (1, 2, 3)]
    soles_b = [sole_b] + [rotated(sole_b, "x", -d) for d in (1, 2, 3)]
    pieces = [[v for both in zip(*part) for v in both] for part in ((packs_a, soles_a), (packs_b, soles_b))]
    packs = [packs_b, packs_a]

    spans = [(64, 1), (512, 1), (512, 4)]
    x = turned
    saved = []
    for n in range(layers):
        span, hops = spans[n]
        if n == 1:
            x = lax.optimization_barrier((x, sole_a))[0]
        received = shifted(x[:, frames - span :], hops)
        late, hidden, slope_f, slope_g, *after = forward(
            n, n + 1 == layers, span, received, x, dilated_weight, current_weight, residual_weight
        )
        saved.append([x, late, hidden, slope_f, slope_g])
        x = after[0] if after else None

    def mixed(jobs):
        return mix(jobs, neg_shard, neg_frame, place, pieces, rows_of, packs)

    near = mixed([[(0, d)] for d in (2, 1, 3)])
    terms = [rotated(v, "x", d) for v, d in zip(near, (2, 1, 3))]
    pieces[1][0], saved[1][2], _ = lax.optimization_barrier((pieces[1][0], saved[1][2], near[0]))
    near = mixed([[(1, d)] for d in (2, 1)])
    terms += [rotated(v, "z", d) for v, d in zip(near, (2, 1))]
    terms.append(rotated(mixed([[(1, 3)]])[0], "z", 3))
    terms.append(mixed([[(0, 0), (1, 0)]])[0])

    halves = [None] * layers
    for n in reversed(range(layers)):
        x, late, hidden, slope_f, slope_g = saved[n]
        span, hops = spans[n]
        grad, dpre, sent = first(n, terms, residual_weight, dilated_weight, slope_f, slope_g)
        received = shifted(sent[:, :span], -hops)
        part, mine, other = rest(n, place, grad, dpre, late, x, hidden, current_weight)
        if n > 0:
            received, other = lax.optimization_barrier((received, other))
        halves[n] = (mine, rotated(other, "c", 1))
        terms = [part, received]
    sums = middle(place, pair(place, *halves[0], *halves[1]), pair(place, *halves[2]))
    keep, away = kernel_call(late_kernel, [like(layers, 16, 5 * chan // 2)] * 2, [place, *sums], [SMEM] + [VMEM] * 8)
    over_both = lax.ppermute(away, ("h", "l"), [(0, 3), (1, 2), (2, 1), (3, 0)])
    ins = [keep, rotated(away, "h", 1), rotated(keep, "l", 1), over_both]
    share = kernel_call(streams_kernel, [like(*keep.shape, dtype=F32)], ins)[0]
    received, share = lax.optimization_barrier((received, share))
    input_grad = kernel_call(functools.partial(final_kernel, span), [like(1, frames, chan)], [part, sent, received])[0]
    outs = [like(layers, 16, n, dtype=F32) for n in (2 * chan, 2 * chan, chan)]
    grads = kernel_call(split_kernel, outs, [place, share, rotated(share, "c", 1)], [SMEM, VMEM, VMEM])
    return (input_grad, *grads)


def solution(mesh):
    fine = Mesh(mesh.devices.reshape(4, 4, 2, 2, 2), ("x", "z", "h", "l", "c"))
    stream = ("l", "c")
    return jax.shard_map(
        on_device,
        mesh=fine,
        in_specs=(P(stream, SEQ, None), P(), P(), P(), P(), P(stream, None, None, SEQ), P(), P()),
        out_specs=(P(stream, SEQ, None), P(None, SEQ, None), P(None, SEQ, None), P(None, SEQ, None)),
        check_vma=False,
    )
```

```python
import functools

import jax
import jax.numpy as jnp
from jax import lax
from jax.experimental import pallas as pl
from jax.experimental.pallas import tpu as pltpu
from jax.sharding import Mesh, PartitionSpec as P

SEQ = ("x", "z", "h")
BF = jnp.bfloat16
F32 = jnp.float32
VMEM = pl.BlockSpec(memory_space=pltpu.VMEM)
SMEM = pl.BlockSpec(memory_space=pltpu.SMEM)
ANY = pl.BlockSpec(memory_space=pl.ANY)
PACE = 1e9


def rotated(value, axis, steps):
    count = lax.axis_size(axis)
    return lax.ppermute(value, axis, [(i, (i + steps) % count) for i in range(count)])


def shifted(value, steps):
    count = 32
    lead, last = (max(0, -steps), min(count, count - steps))
    return lax.ppermute(value, SEQ, [(i, i + steps) for i in range(lead, last)])


def dot(a, b, ca, cb):
    return lax.dot_general(a, b, (((ca,), (cb,)), ((), ())), preferred_element_type=F32)


def like(*shape, dtype=BF):
    return jax.ShapeDtypeStruct(shape, dtype)


def held_for(*weights):
    return [pltpu.VMEM(w.shape[1:], w.dtype) for w in weights] + [pltpu.SemaphoreType.DMA((len(weights),))]


def fetched(n, stacks, held, sems):
    copies = [pltpu.make_async_copy(w.at[n], h, sems.at[m]) for m, (w, h) in enumerate(zip(stacks, held))]
    for copy in copies:
        copy.start()
    return copies


def kernel_call(body, outs, ins, specs=None, scratch=(), limit=12, cost=2.0):
    return pl.pallas_call(
        body,
        out_shape=outs,
        in_specs=specs or [VMEM] * len(ins),
        out_specs=[VMEM] * len(outs),
        scratch_shapes=list(scratch),
        compiler_params=pltpu.CompilerParams(vmem_limit_bytes=limit * 2**20),
        cost_estimate=pl.CostEstimate(flops=int(cost * PACE) + 1, bytes_accessed=1, transcendentals=0),
    )(*ins)


def prepare_kernel(place, features, turned, *blocks):
    frames, rows = turned.shape[1], blocks[0].shape[1]
    for q in range(frames // 128):
        turned[:, q * 128 : (q + 1) * 128] = features[0, q * 128 : (q + 1) * 128, :].T
    for n, block in enumerate(blocks):
        at = pl.multiple_of((n // 4 * 4 + ((place[n // 4] + n % 4) & 3)) * rows, rows)
        for q in range(frames // 128):
            block[q] = turned[pl.ds(at, rows), q * 128 : (q + 1) * 128]


def prepare(place, features):
    _, frames, chan = features.shape
    outs = [like(chan, frames)] + [like(frames // 128, chan // 8, 128)] * 8
    turned, *blocks = kernel_call(prepare_kernel, outs, [place, features], [SMEM, VMEM])
    return turned, blocks[:4], blocks[4:]


def pack_kernel(*refs):
    blocks, logits, outs, wide = (refs[:4], refs[4:8]), refs[8], refs[9:-1], refs[-1]
    steps, width = logits.shape[1:3]
    tiles, rows, _ = blocks[0][0].shape
    for q in range(tiles):
        for k in range(steps):
            at = (q * steps + k) * width
            wide[at : at + width] = logits[0, k, :, q * 128 : (q + 1) * 128]
    for part in range(2):
        pack, sole = outs[part], outs[2 + part]
        for n, block in enumerate(blocks[part]):
            pack[n * tiles : (n + 1) * tiles] = block[...]
            sole[n * tiles : (n + 1) * tiles] = block[...]
        pack[4 * tiles :] = wide[...].astype(BF).reshape(-1, rows, 128)


def pack(blocks_a, blocks_b, logits):
    tiles, rows, _ = blocks_a[0].shape
    held = -(-logits.size // 128 // rows)
    outs = [like(4 * tiles + held, rows, 128)] * 2 + [like(4 * tiles, rows, 128)] * 2
    scratch = [pltpu.VMEM((held * rows, 128), F32)]
    return kernel_call(pack_kernel, outs, [*blocks_a, *blocks_b, logits], scratch=scratch, cost=1.0)


def predict_kernel(place, predict, out_a, out_b, rows, sems):
    steps = sems.shape[1]
    chan = predict.shape[1]
    size = rows.shape[1] // steps
    copies = []
    for part, at in enumerate((place[0], 4 + place[1])):
        for k in range(steps):
            copies.append(
                pltpu.make_async_copy(
                    predict.at[pl.ds(pl.multiple_of(k * chan + at * size, size), size), :],
                    rows.at[part, pl.ds(k * size, size), :],
                    sems.at[part, k],
                )
            )
    for copy in copies:
        copy.start()
    for copy in copies:
        copy.wait()
    out_a[...] = rows[0].T
    out_b[...] = rows[1].T


def mix_kernel(jobs, steps, others, shard, frame, place, *refs):
    parts = sorted({part for job in jobs for part, _ in job})
    order = [pair for job in jobs for pair in job]
    refs = list(refs)
    pieces = {part: [refs.pop(0) for _ in range(8)] for part in parts}
    rows_of = {part: refs.pop(0) for part in parts}
    packs = [refs.pop(0) for _ in order]
    outs = [refs.pop(0) for _ in jobs]
    src, ext, packed, wide, mixed, sems = refs
    count, rows, _ = pieces[parts[0]][1].shape
    tiles = count // 4
    half = rows
    ix, iz, ih = place[0], place[1], place[2]

    def fetch(n):
        size = packed.shape[1]
        return pltpu.make_async_copy(packs[n].at[pl.ds(count, size)], packed.at[n % 2], sems.at[n % 2])

    fetch(0).start()
    for at, part in enumerate(parts):
        for n, piece in enumerate(pieces[part]):
            src[at, n * count : (n + 1) * count] = piece[:count]

    def slot_of(part, index):
        x, z = index >> 3, (index >> 1) & 3
        far, near = (z - iz, ix - x) if part == 0 else (x - ix, iz - z)
        return (((far & 3) * 2 + ((index - ih) & 1)) * 4 + (near & 3)) * tiles

    turn = 0
    for job, out in zip(jobs, outs):
        total = None
        for part, distance in job:
            fetch(turn).wait()
            if turn + 1 < len(order):
                fetch(turn + 1).start()
            wide[...] = packed[turn % 2].reshape(wide.shape).astype(F32)
            turn += 1
            held = src.at[parts.index(part)]
            x, z = ((ix + distance) & 3, iz) if part == 0 else (ix, (iz + distance) & 3)
            target = (x * 4 + z) * 2 + ih
            ext[0:tiles] = held[pl.ds(slot_of(part, target), tiles)]
            after = held[slot_of(part, (target + 1) & 31)]
            ext[tiles] = jnp.where(target < 31, after, jnp.zeros_like(after))

            def step_body(k, carry, part=part, held=held, target=target):
                lane = lax.broadcasted_iota(jnp.int32, (half, 128), 1)
                found = [(slot_of(part, (target + shard[k, j]) & 31), frame[k, j]) for j in range(others)]
                for r in range(rows // half):
                    at = pl.ds(r * half, half)
                    acc = [None] * tiles

                    def add(j, values, f):
                        turned = [pltpu.roll(t, lax.rem(128 - f, 128), 1) for t in values]
                        keep = lane < 128 - f
                        for q in range(tiles):
                            picked = jnp.where(keep, turned[q], turned[(q + 1) % len(values)])
                            weight = jnp.broadcast_to(wide[pl.ds((q * steps + k) * (others + 1) + j, 1), :], (half, 128))
                            term = picked.astype(F32) * weight
                            acc[q] = term if acc[q] is None else acc[q] + term

                    add(0, [ext[q, at, :] for q in range(tiles + 1)], k + 1)
                    for j, (s, at0) in enumerate(found):
                        q0 = lax.shift_right_logical(at0, 7)
                        add(j + 1, [held[s + ((q0 + q) & (tiles - 1)), at, :] for q in range(tiles)], at0 & 127)
                    for q in range(tiles):
                        mixed[pl.ds(pl.multiple_of(k * rows + r * half, half), half), q * 128 : (q + 1) * 128] = acc[q].astype(BF)
                return carry

            lax.fori_loop(0, steps, step_body, 0, unroll=4)
            term = jnp.dot(rows_of[part][...], mixed[...], preferred_element_type=F32)
            total = term if total is None else total + term
        out[...] = total.astype(BF)


def mix(jobs, shard, frame, place, pieces, rows_of, packs):
    parts = sorted({part for job in jobs for part, _ in job})
    steps, others = shard.shape
    chan, depth = rows_of[0].shape
    count, rows, _ = pieces[0][1].shape
    tiles, held = count // 4, packs[0][0].shape[0] - count
    frames = tiles * 128
    scratch = [
        pltpu.VMEM((len(parts), 8 * count, rows, 128), BF),
        pltpu.VMEM((tiles + 1, rows, 128), BF),
        pltpu.VMEM((2, held, rows, 128), BF),
        pltpu.VMEM((held * rows, 128), F32),
        pltpu.VMEM((depth, frames), BF),
        pltpu.SemaphoreType.DMA((2,)),
    ]
    ins = [shard, frame, place] + [v for part in parts for v in pieces[part]] + [rows_of[part] for part in parts]
    last = [packs[part][distance] for job in jobs for part, distance in job]
    body = functools.partial(mix_kernel, jobs, steps, others)
    specs = [SMEM] * 3 + [VMEM] * (len(ins) - 3) + [ANY] * len(last)
    return kernel_call(body, [like(chan, frames)] * len(jobs), ins + last, specs, scratch, limit=16, cost=4.0 * len(last))


def forward_kernel(n, span, last, received, x, *refs):
    stacks, outs, (by_late, by_x, by_hidden, sems) = refs[:3], list(refs[3:-4]), refs[-4:]
    copies = fetched(n, stacks, (by_late, by_x, by_hidden), sems)
    chan, frames = x.shape
    late = received
    if span < frames:
        late = outs.pop(0)
        late[:, :span] = received[...]
        late[:, span:] = x[:, : frames - span]
    hidden, slope_f, slope_g = outs[:3]
    for copy in copies:
        copy.wait()
    filt = jnp.tanh(dot(by_late[:, :chan], late[...], 0, 0) + dot(by_x[:, :chan], x[...], 0, 0))
    pre = dot(by_late[:, chan:], late[...], 0, 0) + dot(by_x[:, chan:], x[...], 0, 0)
    gate = 0.5 * jnp.tanh(0.5 * pre) + 0.5
    out = filt * gate
    hidden[...] = out.astype(BF)
    slope_f[...] = (gate * (1.0 - filt * filt)).astype(BF)
    slope_g[...] = (out * (1.0 - gate)).astype(BF)
    if not last:
        outs[3][...] = (x[...].astype(F32) + dot(by_hidden[...], hidden[...], 0, 0)).astype(BF)


def forward(n, last, span, received, x, by_late, by_x, by_hidden):
    count = (span < x.shape[1]) + 3 + (not last)
    outs = kernel_call(
        functools.partial(forward_kernel, n, span, last),
        [like(*x.shape)] * count,
        [received, x, by_late, by_x, by_hidden],
        [VMEM, VMEM] + [ANY] * 3,
        held_for(by_late, by_x, by_hidden),
        limit=12,
    )
    return outs if span < x.shape[1] else [received] + list(outs)


def first_kernel(n, count, *refs):
    terms, (slope_f, slope_g), stacks = refs[:count], refs[count : count + 2], refs[count + 2 : count + 4]
    grad, dpre, sent, by_hidden, by_late, sems = refs[count + 4 :]
    copies = fetched(n, stacks, (by_hidden, by_late), sems)
    chan = grad.shape[0]
    total = terms[0][...].astype(F32)
    for term in terms[1:]:
        total = total + term[...].astype(F32)
    grad[...] = total.astype(BF)
    copies[0].wait()
    dhid = jnp.dot(by_hidden[...], grad[...], preferred_element_type=F32)
    dpre[:chan] = (dhid * slope_f[...].astype(F32)).astype(BF)
    dpre[chan:] = (dhid * slope_g[...].astype(F32)).astype(BF)
    copies[1].wait()
    sent[...] = jnp.dot(by_late[...], dpre[...], preferred_element_type=F32).astype(BF)


def first(n, terms, by_hidden, by_late, slope_f, slope_g):
    chan, frames = slope_f.shape
    outs = [like(m, frames) for m in (chan, 2 * chan, chan)]
    ins = list(terms) + [slope_f, slope_g, by_hidden, by_late]
    specs = [VMEM] * (len(ins) - 2) + [ANY] * 2
    return kernel_call(functools.partial(first_kernel, n, len(terms)), outs, ins, specs, held_for(by_hidden, by_late))


def rest_kernel(n, place, grad, dpre, late, x, hidden, stack, part, mine, other, by_x, sems):
    chan = x.shape[0]
    copies = fetched(n, (stack,), (by_x,), sems)
    core = place[3]
    for out, at in ((other, 1 - core), (mine, core)):
        rows = dpre[pl.ds(pl.multiple_of(at * chan, chan), chan), :]
        out[:, :chan] = dot(late[...], rows, 1, 1).astype(BF)
        out[:, chan : 2 * chan] = dot(x[...], rows, 1, 1).astype(BF)
        rows = grad[pl.ds(pl.multiple_of(at * (chan // 2), chan // 2), chan // 2), :]
        out[:, 2 * chan :] = dot(hidden[...], rows, 1, 1).astype(BF)
    copies[0].wait()
    part[...] = grad[...].astype(F32) + jnp.dot(by_x[...], dpre[...], preferred_element_type=F32)


def rest(n, place, grad, dpre, late, x, hidden, by_x):
    chan, frames = x.shape
    outs = [like(chan, frames, dtype=F32)] + [like(chan, 5 * chan // 2)] * 2
    specs = [SMEM] + [VMEM] * 5 + [ANY]
    ins = [place, grad, dpre, late, x, hidden, by_x]
    return kernel_call(functools.partial(rest_kernel, n), outs, ins, specs, held_for(by_x))


def pair_kernel(place, *refs):
    values, outs = refs[:-8], refs[-8:]
    count, rows, half = outs[0].shape
    for n in range(count):
        a, b = values[2 * n], values[2 * n + 1]

        def total(at, size, columns):
            span = pl.ds(pl.multiple_of(at, 16), size)
            return (a[span, columns].astype(F32) + b[span, columns].astype(F32)).astype(BF)

        for d in range(4):
            outs[d][n] = total(((place[0] + d) & 3) * rows, rows, slice(0, half))
            size = rows // 4
            for x in range(4):
                outs[4 + d][n, x] = total(x * rows + ((place[1] + d) & 3) * size, size, slice(half, 2 * half))


def pair(place, *values):
    chan, width = values[0].shape
    count, rows, half = len(values) // 2, chan // 4, width // 2
    outs = [like(count, rows, half)] * 4 + [like(count, 4, rows // 4, half)] * 4
    outs = kernel_call(pair_kernel, outs, [place, *values], [SMEM] + [VMEM] * len(values))
    return exchanged(outs, "x", "z")


def exchanged(values, first_axis, second_axis):
    return [
        v if n % 4 == 0 else rotated(v, (first_axis, second_axis)[n // 4], n % 4) for n, v in enumerate(values)
    ]


def middle_kernel(place, *refs):
    groups, outs = (refs[:8], refs[8:16]), refs[16:]
    size = outs[0].shape[1]
    at = 0
    for group in groups:
        for n in range(group[0].shape[0]):
            for d in range(4):
                rows = pl.ds(pl.multiple_of(((place[1] + d) & 3) * size, size), size)
                total = group[0][n, rows, :].astype(F32)
                for m in range(1, 4):
                    total = total + group[m][n, rows, :].astype(F32)
                outs[d][at] = total.astype(BF)
                x = (place[0] + d) & 3
                total = group[4][n, x].astype(F32)
                for m in range(5, 8):
                    total = total + group[m][n, x].astype(F32)
                outs[4 + d][at] = total.astype(BF)
            at += 1


def middle(place, *groups):
    layers = sum(group[0].shape[0] for group in groups)
    _, rows, half = groups[0][0].shape
    ins = [place] + [v for group in groups for v in group]
    outs = kernel_call(middle_kernel, [like(layers, rows // 4, half)] * 8, ins, [SMEM] + [VMEM] * (len(ins) - 1))
    return exchanged(outs, "z", "x")


def late_kernel(place, *refs):
    parts, (keep, away) = refs[:8], refs[8:]
    rows, half = keep.shape[1], parts[0].shape[2]
    for out, h in ((away, 1 - place[2]), (keep, place[2])):
        span = pl.ds(pl.multiple_of(h * rows, rows), rows)
        for side in range(2):
            total = parts[4 * side][:, span, :].astype(F32)
            for m in range(1, 4):
                total = total + parts[4 * side + m][:, span, :].astype(F32)
            out[:, :, side * half : (side + 1) * half] = total.astype(BF)


def streams_kernel(keep, over_h, over_l, over_both, out):
    near = keep[...].astype(F32) + over_h[...].astype(F32)
    out[...] = near + (over_l[...].astype(F32) + over_both[...].astype(F32))


def split_kernel(place, mine, other, *outs):
    core = place[3]
    a, b = mine[...], other[...]
    low, high = jnp.where(core == 0, a, b), jnp.where(core == 0, b, a)
    at = 0
    for out in outs:
        size = out.shape[2] // 2
        out[:, :, :size] = low[:, :, at : at + size]
        out[:, :, size:] = high[:, :, at : at + size]
        at += size


def final_kernel(span, part, sent, received, out):
    chan, frames = part.shape
    total = (part[:, : frames - span] + sent[:, span:].astype(F32)).astype(BF)
    out[0, : frames - span] = total.T
    total = (part[:, frames - span :] + received[...].astype(F32)).astype(BF)
    out[0, frames - span :] = total.T


def on_device(features, dilated_weight, current_weight, residual_weight, predict, logit_grads, neg_shard, neg_frame):
    _, frames, chan = features.shape
    layers = dilated_weight.shape[0]
    steps, others = neg_shard.shape
    rows = chan // 8
    place = jnp.stack([lax.axis_index(a) for a in ("x", "z", "h", "c")])

    turned, blocks_a, blocks_b = prepare(place, features)
    rows_of = kernel_call(
        predict_kernel,
        [like(chan, steps * rows)] * 2,
        [place, predict],
        [SMEM, ANY],
        [pltpu.VMEM((2, steps * rows, chan), BF), pltpu.SemaphoreType.DMA((2, steps))],
        cost=4.0,
    )
    blocks_a = blocks_a[:1] + [rotated(blocks_a[d], "x", d) for d in (1, 2, 3)]
    blocks_b = blocks_b[:1] + [rotated(blocks_b[d], "z", d) for d in (1, 2, 3)]
    blocks_a, rows_of = lax.optimization_barrier((blocks_a, rows_of))
    pack_a, pack_b, sole_a, sole_b = pack(blocks_a, blocks_b, logit_grads)
    sole_a, sole_b = rotated(sole_a, "h", 1), rotated(sole_b, "h", 1)
    packs_a = [pack_a] + [rotated(pack_a, "z", -d) for d in (1, 2, 3)]
    packs_b = [pack_b] + [rotated(pack_b, "x", -d) for d in (1, 2, 3)]
    soles_a = [sole_a] + [rotated(sole_a, "z", -d) for d in (1, 2, 3)]
    soles_b = [sole_b] + [rotated(sole_b, "x", -d) for d in (1, 2, 3)]
    pieces = [[v for both in zip(*part) for v in both] for part in ((packs_a, soles_a), (packs_b, soles_b))]
    packs = [packs_b, packs_a]

    spans = [(64, 1), (512, 1), (512, 4)]
    x = turned
    saved = []
    for n in range(layers):
        span, hops = spans[n]
        if n == 1:
            x = lax.optimization_barrier((x, sole_a))[0]
        received = shifted(x[:, frames - span :], hops)
        late, hidden, slope_f, slope_g, *after = forward(
            n, n + 1 == layers, span, received, x, dilated_weight, current_weight, residual_weight
        )
        saved.append([x, late, hidden, slope_f, slope_g])
        x = after[0] if after else None

    def mixed(jobs):
        return mix(jobs, neg_shard, neg_frame, place, pieces, rows_of, packs)

    near = mixed([[(0, d)] for d in (2, 1, 3)])
    terms = [rotated(v, "x", d) for v, d in zip(near, (2, 1, 3))]
    pieces[1][0], saved[1][2], _ = lax.optimization_barrier((pieces[1][0], saved[1][2], near[0]))
    near = mixed([[(1, d)] for d in (2, 1)])
    terms += [rotated(v, "z", d) for v, d in zip(near, (2, 1))]
    terms.append(rotated(mixed([[(1, 3)]])[0], "z", 3))
    terms.append(mixed([[(0, 0), (1, 0)]])[0])

    halves = [None] * layers
    for n in reversed(range(layers)):
        x, late, hidden, slope_f, slope_g = saved[n]
        span, hops = spans[n]
        grad, dpre, sent = first(n, terms, residual_weight, dilated_weight, slope_f, slope_g)
        received = shifted(sent[:, :span], -hops)
        part, mine, other = rest(n, place, grad, dpre, late, x, hidden, current_weight)
        if n > 0:
            received, other = lax.optimization_barrier((received, other))
        halves[n] = (mine, rotated(other, "c", 1))
        terms = [part, received]
    sums = middle(place, pair(place, *halves[0], *halves[1]), pair(place, *halves[2]))
    keep, away = kernel_call(late_kernel, [like(layers, 16, 5 * chan // 2)] * 2, [place, *sums], [SMEM] + [VMEM] * 8)
    over_both = lax.ppermute(away, ("h", "l"), [(0, 3), (1, 2), (2, 1), (3, 0)])
    ins = [keep, rotated(away, "h", 1), rotated(keep, "l", 1), over_both]
    share = kernel_call(streams_kernel, [like(*keep.shape, dtype=F32)], ins)[0]
    received, share = lax.optimization_barrier((received, share))
    input_grad = kernel_call(functools.partial(final_kernel, span), [like(1, frames, chan)], [part, sent, received])[0]
    outs = [like(layers, 16, n, dtype=F32) for n in (2 * chan, 2 * chan, chan)]
    grads = kernel_call(split_kernel, outs, [place, share, rotated(share, "c", 1)], [SMEM, VMEM, VMEM])
    return (input_grad, *grads)


def solution(mesh):
    fine = Mesh(mesh.devices.reshape(4, 4, 2, 2, 2), ("x", "z", "h", "l", "c"))
    stream = ("l", "c")
    return jax.shard_map(
        on_device,
        mesh=fine,
        in_specs=(P(stream, SEQ, None), P(), P(), P(), P(), P(stream, None, None, SEQ), P(), P()),
        out_specs=(P(stream, SEQ, None), P(None, SEQ, None), P(None, SEQ, None), P(None, SEQ, None)),
        check_vma=False,
    )
```

```python
import functools

import jax
import jax.numpy as jnp
from jax import lax
from jax.experimental import pallas as pl
from jax.experimental.pallas import tpu as pltpu
from jax.sharding import Mesh, PartitionSpec as P

SEQ = ("x", "z", "h")
BF = jnp.bfloat16
F32 = jnp.float32
VMEM = pl.BlockSpec(memory_space=pltpu.VMEM)
SMEM = pl.BlockSpec(memory_space=pltpu.SMEM)
ANY = pl.BlockSpec(memory_space=pl.ANY)
PACE = 1e9


def rotated(value, axis, steps):
    count = lax.axis_size(axis)
    return lax.ppermute(value, axis, [(i, (i + steps) % count) for i in range(count)])


def shifted(value, steps):
    count = 32
    lead, last = (max(0, -steps), min(count, count - steps))
    return lax.ppermute(value, SEQ, [(i, i + steps) for i in range(lead, last)])


def dot(a, b, ca, cb):
    return lax.dot_general(a, b, (((ca,), (cb,)), ((), ())), preferred_element_type=F32)


def like(*shape, dtype=BF):
    return jax.ShapeDtypeStruct(shape, dtype)


def held_for(*weights):
    return [pltpu.VMEM(w.shape[1:], w.dtype) for w in weights] + [pltpu.SemaphoreType.DMA((len(weights),))]


def fetched(n, stacks, held, sems):
    copies = [pltpu.make_async_copy(w.at[n], h, sems.at[m]) for m, (w, h) in enumerate(zip(stacks, held))]
    for copy in copies:
        copy.start()
    return copies


def kernel_call(body, outs, ins, specs=None, scratch=(), limit=12, cost=2.0):
    return pl.pallas_call(
        body,
        out_shape=outs,
        in_specs=specs or [VMEM] * len(ins),
        out_specs=[VMEM] * len(outs),
        scratch_shapes=list(scratch),
        compiler_params=pltpu.CompilerParams(vmem_limit_bytes=limit * 2**20),
        cost_estimate=pl.CostEstimate(flops=int(cost * PACE) + 1, bytes_accessed=1, transcendentals=0),
    )(*ins)


def prepare_kernel(place, features, turned, *blocks):
    frames, rows = turned.shape[1], blocks[0].shape[1]
    for q in range(frames // 128):
        turned[:, q * 128 : (q + 1) * 128] = features[0, q * 128 : (q + 1) * 128, :].T
    for n, block in enumerate(blocks):
        at = pl.multiple_of((n // 4 * 4 + ((place[n // 4] + n % 4) & 3)) * rows, rows)
        for q in range(frames // 128):
            block[q] = turned[pl.ds(at, rows), q * 128 : (q + 1) * 128]


def prepare(place, features):
    _, frames, chan = features.shape
    outs = [like(chan, frames)] + [like(frames // 128, chan // 8, 128)] * 8
    turned, *blocks = kernel_call(prepare_kernel, outs, [place, features], [SMEM, VMEM])
    return turned, blocks[:4], blocks[4:]


def pack_kernel(*refs):
    blocks, logits, outs, wide = (refs[:4], refs[4:8]), refs[8], refs[9:-1], refs[-1]
    steps, width = logits.shape[1:3]
    tiles, rows, _ = blocks[0][0].shape
    for q in range(tiles):
        for k in range(steps):
            at = (q * steps + k) * width
            wide[at : at + width] = logits[0, k, :, q * 128 : (q + 1) * 128]
    for part in range(2):
        pack, sole = outs[part], outs[2 + part]
        for n, block in enumerate(blocks[part]):
            pack[n * tiles : (n + 1) * tiles] = block[...]
            sole[n * tiles : (n + 1) * tiles] = block[...]
        pack[4 * tiles :] = wide[...].astype(BF).reshape(-1, rows, 128)


def pack(blocks_a, blocks_b, logits):
    tiles, rows, _ = blocks_a[0].shape
    held = -(-logits.size // 128 // rows)
    outs = [like(4 * tiles + held, rows, 128)] * 2 + [like(4 * tiles, rows, 128)] * 2
    scratch = [pltpu.VMEM((held * rows, 128), F32)]
    return kernel_call(pack_kernel, outs, [*blocks_a, *blocks_b, logits], scratch=scratch, cost=1.0)


def predict_kernel(place, predict, out_a, out_b, rows, sems):
    steps = sems.shape[1]
    chan = predict.shape[1]
    size = rows.shape[1] // steps
    copies = []
    for part, at in enumerate((place[0], 4 + place[1])):
        for k in range(steps):
            copies.append(
                pltpu.make_async_copy(
                    predict.at[pl.ds(pl.multiple_of(k * chan + at * size, size), size), :],
                    rows.at[part, pl.ds(k * size, size), :],
                    sems.at[part, k],
                )
            )
    for copy in copies:
        copy.start()
    for copy in copies:
        copy.wait()
    out_a[...] = rows[0].T
    out_b[...] = rows[1].T


def mix_kernel(jobs, steps, others, shard, frame, place, *refs):
    parts = sorted({part for job in jobs for part, _ in job})
    order = [pair for job in jobs for pair in job]
    refs = list(refs)
    pieces = {part: [refs.pop(0) for _ in range(8)] for part in parts}
    rows_of = {part: refs.pop(0) for part in parts}
    packs = [refs.pop(0) for _ in order]
    outs = [refs.pop(0) for _ in jobs]
    src, ext, packed, wide, mixed, sems = refs
    count, rows, _ = pieces[parts[0]][1].shape
    tiles = count // 4
    half = rows
    ix, iz, ih = place[0], place[1], place[2]

    def fetch(n):
        size = packed.shape[1]
        return pltpu.make_async_copy(packs[n].at[pl.ds(count, size)], packed.at[n % 2], sems.at[n % 2])

    fetch(0).start()
    for at, part in enumerate(parts):
        for n, piece in enumerate(pieces[part]):
            src[at, n * count : (n + 1) * count] = piece[:count]

    def slot_of(part, index):
        x, z = index >> 3, (index >> 1) & 3
        far, near = (z - iz, ix - x) if part == 0 else (x - ix, iz - z)
        return (((far & 3) * 2 + ((index - ih) & 1)) * 4 + (near & 3)) * tiles

    turn = 0
    for job, out in zip(jobs, outs):
        total = None
        for part, distance in job:
            fetch(turn).wait()
            if turn + 1 < len(order):
                fetch(turn + 1).start()
            wide[...] = packed[turn % 2].reshape(wide.shape).astype(F32)
            turn += 1
            held = src.at[parts.index(part)]
            x, z = ((ix + distance) & 3, iz) if part == 0 else (ix, (iz + distance) & 3)
            target = (x * 4 + z) * 2 + ih
            ext[0:tiles] = held[pl.ds(slot_of(part, target), tiles)]
            after = held[slot_of(part, (target + 1) & 31)]
            ext[tiles] = jnp.where(target < 31, after, jnp.zeros_like(after))

            def step_body(k, carry, part=part, held=held, target=target):
                lane = lax.broadcasted_iota(jnp.int32, (half, 128), 1)
                found = [(slot_of(part, (target + shard[k, j]) & 31), frame[k, j]) for j in range(others)]
                for r in range(rows // half):
                    at = pl.ds(r * half, half)
                    acc = [None] * tiles

                    def add(j, values, f):
                        turned = [pltpu.roll(t, lax.rem(128 - f, 128), 1) for t in values]
                        keep = lane < 128 - f
                        for q in range(tiles):
                            picked = jnp.where(keep, turned[q], turned[(q + 1) % len(values)])
                            weight = jnp.broadcast_to(wide[pl.ds((q * steps + k) * (others + 1) + j, 1), :], (half, 128))
                            term = picked.astype(F32) * weight
                            acc[q] = term if acc[q] is None else acc[q] + term

                    add(0, [ext[q, at, :] for q in range(tiles + 1)], k + 1)
                    for j, (s, at0) in enumerate(found):
                        q0 = lax.shift_right_logical(at0, 7)
                        add(j + 1, [held[s + ((q0 + q) & (tiles - 1)), at, :] for q in range(tiles)], at0 & 127)
                    for q in range(tiles):
                        mixed[pl.ds(pl.multiple_of(k * rows + r * half, half), half), q * 128 : (q + 1) * 128] = acc[q].astype(BF)
                return carry

            lax.fori_loop(0, steps, step_body, 0, unroll=4)
            term = jnp.dot(rows_of[part][...], mixed[...], preferred_element_type=F32)
            total = term if total is None else total + term
        out[...] = total.astype(BF)


def mix(jobs, shard, frame, place, pieces, rows_of, packs):
    parts = sorted({part for job in jobs for part, _ in job})
    steps, others = shard.shape
    chan, depth = rows_of[0].shape
    count, rows, _ = pieces[0][1].shape
    tiles, held = count // 4, packs[0][0].shape[0] - count
    frames = tiles * 128
    scratch = [
        pltpu.VMEM((len(parts), 8 * count, rows, 128), BF),
        pltpu.VMEM((tiles + 1, rows, 128), BF),
        pltpu.VMEM((2, held, rows, 128), BF),
        pltpu.VMEM((held * rows, 128), F32),
        pltpu.VMEM((depth, frames), BF),
        pltpu.SemaphoreType.DMA((2,)),
    ]
    ins = [shard, frame, place] + [v for part in parts for v in pieces[part]] + [rows_of[part] for part in parts]
    last = [packs[part][distance] for job in jobs for part, distance in job]
    body = functools.partial(mix_kernel, jobs, steps, others)
    specs = [SMEM] * 3 + [VMEM] * (len(ins) - 3) + [ANY] * len(last)
    return kernel_call(body, [like(chan, frames)] * len(jobs), ins + last, specs, scratch, limit=16, cost=4.0 * len(last))


def forward_kernel(n, span, last, received, x, *refs):
    stacks, outs, (by_late, by_x, by_hidden, sems) = refs[:3], list(refs[3:-4]), refs[-4:]
    copies = fetched(n, stacks, (by_late, by_x, by_hidden), sems)
    chan, frames = x.shape
    late = received
    if span < frames:
        late = outs.pop(0)
        late[:, :span] = received[...]
        late[:, span:] = x[:, : frames - span]
    hidden, slope_f, slope_g = outs[:3]
    for copy in copies:
        copy.wait()
    filt = jnp.tanh(dot(by_late[:, :chan], late[...], 0, 0) + dot(by_x[:, :chan], x[...], 0, 0))
    pre = dot(by_late[:, chan:], late[...], 0, 0) + dot(by_x[:, chan:], x[...], 0, 0)
    gate = 0.5 * jnp.tanh(0.5 * pre) + 0.5
    out = filt * gate
    hidden[...] = out.astype(BF)
    slope_f[...] = (gate * (1.0 - filt * filt)).astype(BF)
    slope_g[...] = (out * (1.0 - gate)).astype(BF)
    if not last:
        outs[3][...] = (x[...].astype(F32) + dot(by_hidden[...], hidden[...], 0, 0)).astype(BF)


def forward(n, last, span, received, x, by_late, by_x, by_hidden):
    count = (span < x.shape[1]) + 3 + (not last)
    outs = kernel_call(
        functools.partial(forward_kernel, n, span, last),
        [like(*x.shape)] * count,
        [received, x, by_late, by_x, by_hidden],
        [VMEM, VMEM] + [ANY] * 3,
        held_for(by_late, by_x, by_hidden),
        limit=12,
    )
    return outs if span < x.shape[1] else [received] + list(outs)


def first_kernel(n, count, *refs):
    terms, (slope_f, slope_g), stacks = refs[:count], refs[count : count + 2], refs[count + 2 : count + 4]
    grad, dpre, sent, by_hidden, by_late, sems = refs[count + 4 :]
    copies = fetched(n, stacks, (by_hidden, by_late), sems)
    chan = grad.shape[0]
    total = terms[0][...].astype(F32)
    for term in terms[1:]:
        total = total + term[...].astype(F32)
    grad[...] = total.astype(BF)
    copies[0].wait()
    dhid = jnp.dot(by_hidden[...], grad[...], preferred_element_type=F32)
    dpre[:chan] = (dhid * slope_f[...].astype(F32)).astype(BF)
    dpre[chan:] = (dhid * slope_g[...].astype(F32)).astype(BF)
    copies[1].wait()
    sent[...] = jnp.dot(by_late[...], dpre[...], preferred_element_type=F32).astype(BF)


def first(n, terms, by_hidden, by_late, slope_f, slope_g):
    chan, frames = slope_f.shape
    outs = [like(m, frames) for m in (chan, 2 * chan, chan)]
    ins = list(terms) + [slope_f, slope_g, by_hidden, by_late]
    specs = [VMEM] * (len(ins) - 2) + [ANY] * 2
    return kernel_call(functools.partial(first_kernel, n, len(terms)), outs, ins, specs, held_for(by_hidden, by_late))


def rest_kernel(n, place, grad, dpre, late, x, hidden, stack, part, mine, other, by_x, sems):
    chan = x.shape[0]
    copies = fetched(n, (stack,), (by_x,), sems)
    core = place[3]
    for out, at in ((other, 1 - core), (mine, core)):
        rows = dpre[pl.ds(pl.multiple_of(at * chan, chan), chan), :]
        out[:, :chan] = dot(late[...], rows, 1, 1).astype(BF)
        out[:, chan : 2 * chan] = dot(x[...], rows, 1, 1).astype(BF)
        rows = grad[pl.ds(pl.multiple_of(at * (chan // 2), chan // 2), chan // 2), :]
        out[:, 2 * chan :] = dot(hidden[...], rows, 1, 1).astype(BF)
    copies[0].wait()
    part[...] = grad[...].astype(F32) + jnp.dot(by_x[...], dpre[...], preferred_element_type=F32)


def rest(n, place, grad, dpre, late, x, hidden, by_x):
    chan, frames = x.shape
    outs = [like(chan, frames, dtype=F32)] + [like(chan, 5 * chan // 2)] * 2
    specs = [SMEM] + [VMEM] * 5 + [ANY]
    ins = [place, grad, dpre, late, x, hidden, by_x]
    return kernel_call(functools.partial(rest_kernel, n), outs, ins, specs, held_for(by_x))


def pair_kernel(place, *refs):
    values, outs = refs[:-10], refs[-10:]
    count, rows, half = outs[0].shape
    for n in range(count):
        a, b = values[2 * n], values[2 * n + 1]

        def total(at, size, columns):
            span = pl.ds(pl.multiple_of(at, 16), size)
            return (a[span, columns].astype(F32) + b[span, columns].astype(F32)).astype(BF)

        for d in (0, 1, 3):
            outs[(0, 1, None, 2)[d]][n] = total(((place[0] + d) & 3) * rows, rows, slice(0, half))
        far = ((place[0] + 2) & 3) * rows
        for m in range(2):
            outs[3 + m][n] = total(far + m * (rows // 2), rows // 2, slice(0, half))
        size = rows // 4
        for x in range(4):
            for d in (0, 1, 3):
                outs[5 + (0, 1, None, 2)[d]][n, x] = total(x * rows + ((place[1] + d) & 3) * size, size, slice(half, 2 * half))
            outs[8 + x // 2][n, x % 2] = total(x * rows + ((place[1] + 2) & 3) * size, size, slice(half, 2 * half))


def relay_kernel(*refs):
    (up, down, from_low, from_high), outs = refs[:4], refs[4:6]
    half = from_low.shape[1]
    for n in range(up.shape[0]):
        outs[0][n, :half] = (up[n, :half].astype(F32) + from_low[n].astype(F32)).astype(BF)
        outs[0][n, half:] = up[n, half:]
        outs[1][n, :half] = down[n, :half]
        outs[1][n, half:] = (down[n, half:].astype(F32) + from_high[n].astype(F32)).astype(BF)


def relay(values, axis):
    own, up, down, first_half, second_half = values
    ins = [up, down, rotated(first_half, axis, 1), rotated(second_half, axis, -1)]
    up, down = kernel_call(relay_kernel, [like(*up.shape)] * 2, ins, cost=1.0)
    return [own, rotated(up, axis, 1), rotated(down, axis, -1)]


def pair(place, *values):
    chan, width = values[0].shape
    count, rows, half = len(values) // 2, chan // 4, width // 2
    outs = [like(count, rows, half)] * 3 + [like(count, rows // 2, half)] * 2
    outs += [like(count, 4, rows // 4, half)] * 3 + [like(count, 2, rows // 4, half)] * 2
    outs = kernel_call(pair_kernel, outs, [place, *values], [SMEM] + [VMEM] * len(values), cost=1.5)
    return relay(outs[:5], "x") + relay(outs[5:], "z")


def exchanged(values, first_axis, second_axis):
    return [
        v if n % 4 == 0 else rotated(v, (first_axis, second_axis)[n // 4], n % 4) for n, v in enumerate(values)
    ]


def middle_kernel(place, *refs):
    groups, outs = [refs[n : n + 6] for n in range(0, len(refs) - 8, 6)], refs[-8:]
    size = outs[0].shape[1]
    at = 0
    for group in groups:
        for n in range(group[0].shape[0]):
            for d in range(4):
                rows = pl.ds(pl.multiple_of(((place[1] + d) & 3) * size, size), size)
                total = group[0][n, rows, :].astype(F32)
                for m in range(1, 3):
                    total = total + group[m][n, rows, :].astype(F32)
                outs[d][at] = total.astype(BF)
                x = (place[0] + d) & 3
                total = group[3][n, x].astype(F32)
                for m in range(4, 6):
                    total = total + group[m][n, x].astype(F32)
                outs[4 + d][at] = total.astype(BF)
            at += 1


def middle(place, *groups):
    layers = sum(group[0].shape[0] for group in groups)
    _, rows, half = groups[0][0].shape
    ins = [place] + [v for group in groups for v in group]
    outs = kernel_call(middle_kernel, [like(layers, rows // 4, half)] * 8, ins, [SMEM] + [VMEM] * (len(ins) - 1))
    return exchanged(outs, "z", "x")


def late_kernel(place, *refs):
    parts, (keep, away) = refs[:8], refs[8:]
    rows, half = keep.shape[1], parts[0].shape[2]
    for out, h in ((away, 1 - place[2]), (keep, place[2])):
        span = pl.ds(pl.multiple_of(h * rows, rows), rows)
        for side in range(2):
            total = parts[4 * side][:, span, :].astype(F32)
            for m in range(1, 4):
                total = total + parts[4 * side + m][:, span, :].astype(F32)
            out[:, :, side * half : (side + 1) * half] = total.astype(BF)


def streams_kernel(keep, over_h, over_l, over_both, out):
    near = keep[...].astype(F32) + over_h[...].astype(F32)
    out[...] = near + (over_l[...].astype(F32) + over_both[...].astype(F32))


def split_kernel(place, mine, other, *outs):
    core = place[3]
    a, b = mine[...], other[...]
    low, high = jnp.where(core == 0, a, b), jnp.where(core == 0, b, a)
    at = 0
    for out in outs:
        size = out.shape[2] // 2
        out[:, :, :size] = low[:, :, at : at + size]
        out[:, :, size:] = high[:, :, at : at + size]
        at += size


def final_kernel(span, part, sent, received, out):
    chan, frames = part.shape
    total = (part[:, : frames - span] + sent[:, span:].astype(F32)).astype(BF)
    out[0, : frames - span] = total.T
    total = (part[:, frames - span :] + received[...].astype(F32)).astype(BF)
    out[0, frames - span :] = total.T


def on_device(features, dilated_weight, current_weight, residual_weight, predict, logit_grads, neg_shard, neg_frame):
    _, frames, chan = features.shape
    layers = dilated_weight.shape[0]
    steps, others = neg_shard.shape
    rows = chan // 8
    place = jnp.stack([lax.axis_index(a) for a in ("x", "z", "h", "c")])

    turned, blocks_a, blocks_b = prepare(place, features)
    rows_of = kernel_call(
        predict_kernel,
        [like(chan, steps * rows)] * 2,
        [place, predict],
        [SMEM, ANY],
        [pltpu.VMEM((2, steps * rows, chan), BF), pltpu.SemaphoreType.DMA((2, steps))],
        cost=4.0,
    )
    blocks_a = blocks_a[:1] + [rotated(blocks_a[d], "x", d) for d in (1, 2, 3)]
    blocks_b = blocks_b[:1] + [rotated(blocks_b[d], "z", d) for d in (1, 2, 3)]
    blocks_a, rows_of = lax.optimization_barrier((blocks_a, rows_of))
    pack_a, pack_b, sole_a, sole_b = pack(blocks_a, blocks_b, logit_grads)
    sole_a, sole_b = rotated(sole_a, "h", 1), rotated(sole_b, "h", 1)
    packs_a = [pack_a] + [rotated(pack_a, "z", -d) for d in (1, 2, 3)]
    packs_b = [pack_b] + [rotated(pack_b, "x", -d) for d in (1, 2, 3)]
    soles_a = [sole_a] + [rotated(sole_a, "z", -d) for d in (1, 2, 3)]
    soles_b = [sole_b] + [rotated(sole_b, "x", -d) for d in (1, 2, 3)]
    pieces = [[v for both in zip(*part) for v in both] for part in ((packs_a, soles_a), (packs_b, soles_b))]
    packs = [packs_b, packs_a]

    spans = [(64, 1), (512, 1), (512, 4)]
    x = turned
    saved = []
    for n in range(layers):
        span, hops = spans[n]
        if n == 1:
            x = lax.optimization_barrier((x, sole_a))[0]
        received = shifted(x[:, frames - span :], hops)
        late, hidden, slope_f, slope_g, *after = forward(
            n, n + 1 == layers, span, received, x, dilated_weight, current_weight, residual_weight
        )
        saved.append([x, late, hidden, slope_f, slope_g])
        x = after[0] if after else None

    def mixed(jobs):
        return mix(jobs, neg_shard, neg_frame, place, pieces, rows_of, packs)

    near = mixed([[(0, d)] for d in (2, 1, 3)])
    terms = [rotated(v, "x", d) for v, d in zip(near, (2, 1, 3))]
    pieces[1][0], saved[1][2], _ = lax.optimization_barrier((pieces[1][0], saved[1][2], near[0]))
    near = mixed([[(1, d)] for d in (2, 1)])
    terms += [rotated(v, "z", d) for v, d in zip(near, (2, 1))]
    terms.append(rotated(mixed([[(1, 3)]])[0], "z", 3))
    terms.append(mixed([[(0, 0), (1, 0)]])[0])

    halves = [None] * layers
    for n in reversed(range(layers)):
        x, late, hidden, slope_f, slope_g = saved[n]
        span, hops = spans[n]
        grad, dpre, sent = first(n, terms, residual_weight, dilated_weight, slope_f, slope_g)
        received = shifted(sent[:, :span], -hops)
        part, mine, other = rest(n, place, grad, dpre, late, x, hidden, current_weight)
        if n > 0:
            received, other = lax.optimization_barrier((received, other))
        halves[n] = (mine, rotated(other, "c", 1))
        terms = [part, received]
    sums = middle(place, pair(place, *halves[0], *halves[1], *halves[2]))
    keep, away = kernel_call(late_kernel, [like(layers, 16, 5 * chan // 2)] * 2, [place, *sums], [SMEM] + [VMEM] * 8)
    over_both = lax.ppermute(away, ("h", "l"), [(0, 3), (1, 2), (2, 1), (3, 0)])
    ins = [keep, rotated(away, "h", 1), rotated(keep, "l", 1), over_both]
    share = kernel_call(streams_kernel, [like(*keep.shape, dtype=F32)], ins)[0]
    received, share = lax.optimization_barrier((received, share))
    input_grad = kernel_call(functools.partial(final_kernel, span), [like(1, frames, chan)], [part, sent, received])[0]
    outs = [like(layers, 16, n, dtype=F32) for n in (2 * chan, 2 * chan, chan)]
    grads = kernel_call(split_kernel, outs, [place, share, rotated(share, "c", 1)], [SMEM, VMEM, VMEM])
    return (input_grad, *grads)


def solution(mesh):
    fine = Mesh(mesh.devices.reshape(4, 4, 2, 2, 2), ("x", "z", "h", "l", "c"))
    stream = ("l", "c")
    return jax.shard_map(
        on_device,
        mesh=fine,
        in_specs=(P(stream, SEQ, None), P(), P(), P(), P(), P(stream, None, None, SEQ), P(), P()),
        out_specs=(P(stream, SEQ, None), P(None, SEQ, None), P(None, SEQ, None), P(None, SEQ, None)),
        check_vma=False,
    )
```

```python
import functools

import jax
import jax.numpy as jnp
from jax import lax
from jax.experimental import pallas as pl
from jax.experimental.pallas import tpu as pltpu
from jax.sharding import Mesh, PartitionSpec as P

SEQ = ("x", "z", "h")
BF = jnp.bfloat16
F32 = jnp.float32
VMEM = pl.BlockSpec(memory_space=pltpu.VMEM)
SMEM = pl.BlockSpec(memory_space=pltpu.SMEM)
ANY = pl.BlockSpec(memory_space=pl.ANY)
PACE = 2e9


def rotated(value, axis, steps):
    count = lax.axis_size(axis)
    return lax.ppermute(value, axis, [(i, (i + steps) % count) for i in range(count)])


def shifted(value, steps):
    count = 32
    lead, last = (max(0, -steps), min(count, count - steps))
    return lax.ppermute(value, SEQ, [(i, i + steps) for i in range(lead, last)])


def dot(a, b, ca, cb):
    return lax.dot_general(a, b, (((ca,), (cb,)), ((), ())), preferred_element_type=F32)


def like(*shape, dtype=BF):
    return jax.ShapeDtypeStruct(shape, dtype)


def held_for(*weights):
    return [pltpu.VMEM(w.shape[1:], w.dtype) for w in weights] + [pltpu.SemaphoreType.DMA((len(weights),))]


def fetched(n, stacks, held, sems):
    copies = [pltpu.make_async_copy(w.at[n], h, sems.at[m]) for m, (w, h) in enumerate(zip(stacks, held))]
    for copy in copies:
        copy.start()
    return copies


def kernel_call(body, outs, ins, specs=None, scratch=(), limit=12, cost=2.0):
    return pl.pallas_call(
        body,
        out_shape=outs,
        in_specs=specs or [VMEM] * len(ins),
        out_specs=[VMEM] * len(outs),
        scratch_shapes=list(scratch),
        compiler_params=pltpu.CompilerParams(vmem_limit_bytes=limit * 2**20),
        cost_estimate=pl.CostEstimate(flops=int(cost * PACE) + 1, bytes_accessed=1, transcendentals=0),
    )(*ins)


def prepare_kernel(place, features, turned, *blocks):
    frames, rows = turned.shape[1], blocks[0].shape[1]
    for q in range(frames // 128):
        turned[:, q * 128 : (q + 1) * 128] = features[0, q * 128 : (q + 1) * 128, :].T
    for n, block in enumerate(blocks):
        at = pl.multiple_of((n // 4 * 4 + ((place[n // 4] + n % 4) & 3)) * rows, rows)
        for q in range(frames // 128):
            block[q] = turned[pl.ds(at, rows), q * 128 : (q + 1) * 128]


def prepare(place, features):
    _, frames, chan = features.shape
    outs = [like(chan, frames)] + [like(frames // 128, chan // 8, 128)] * 8
    turned, *blocks = kernel_call(prepare_kernel, outs, [place, features], [SMEM, VMEM])
    return turned, blocks[:4], blocks[4:]


def pack_kernel(*refs):
    blocks, logits, outs, wide = (refs[:4], refs[4:8]), refs[8], refs[9:-1], refs[-1]
    steps, width = logits.shape[1:3]
    tiles, rows, _ = blocks[0][0].shape
    for q in range(tiles):
        for k in range(steps):
            at = (q * steps + k) * width
            wide[at : at + width] = logits[0, k, :, q * 128 : (q + 1) * 128]
    for part in range(2):
        pack, sole = outs[part], outs[2 + part]
        for n, block in enumerate(blocks[part]):
            pack[n * tiles : (n + 1) * tiles] = block[...]
            sole[n * tiles : (n + 1) * tiles] = block[...]
        pack[4 * tiles :] = wide[...].astype(BF).reshape(-1, rows, 128)


def pack(blocks_a, blocks_b, logits):
    tiles, rows, _ = blocks_a[0].shape
    held = -(-logits.size // 128 // rows)
    outs = [like(4 * tiles + held, rows, 128)] * 2 + [like(4 * tiles, rows, 128)] * 2
    scratch = [pltpu.VMEM((held * rows, 128), F32)]
    return kernel_call(pack_kernel, outs, [*blocks_a, *blocks_b, logits], scratch=scratch, cost=1.0)


def predict_kernel(place, predict, out_a, out_b, rows, sems):
    steps = sems.shape[1]
    chan = predict.shape[1]
    size = rows.shape[1] // steps
    copies = []
    for part, at in enumerate((place[0], 4 + place[1])):
        for k in range(steps):
            copies.append(
                pltpu.make_async_copy(
                    predict.at[pl.ds(pl.multiple_of(k * chan + at * size, size), size), :],
                    rows.at[part, pl.ds(k * size, size), :],
                    sems.at[part, k],
                )
            )
    for copy in copies:
        copy.start()
    for copy in copies:
        copy.wait()
    out_a[...] = rows[0].T
    out_b[...] = rows[1].T


def mix_kernel(jobs, steps, others, shard, frame, place, *refs):
    parts = sorted({part for job in jobs for part, _ in job})
    order = [pair for job in jobs for pair in job]
    refs = list(refs)
    pieces = {part: [refs.pop(0) for _ in range(8)] for part in parts}
    rows_of = {part: refs.pop(0) for part in parts}
    packs = [refs.pop(0) for _ in order]
    outs = [refs.pop(0) for _ in jobs]
    src, ext, packed, wide, mixed, sems = refs
    count, rows, _ = pieces[parts[0]][1].shape
    tiles = count // 4
    half = rows
    ix, iz, ih = place[0], place[1], place[2]

    def fetch(n):
        size = packed.shape[1]
        return pltpu.make_async_copy(packs[n].at[pl.ds(count, size)], packed.at[n % 2], sems.at[n % 2])

    fetch(0).start()
    for at, part in enumerate(parts):
        for n, piece in enumerate(pieces[part]):
            src[at, n * count : (n + 1) * count] = piece[:count]

    def slot_of(part, index):
        x, z = index >> 3, (index >> 1) & 3
        far, near = (z - iz, ix - x) if part == 0 else (x - ix, iz - z)
        return (((far & 3) * 2 + ((index - ih) & 1)) * 4 + (near & 3)) * tiles

    turn = 0
    for job, out in zip(jobs, outs):
        total = None
        for part, distance in job:
            fetch(turn).wait()
            if turn + 1 < len(order):
                fetch(turn + 1).start()
            wide[...] = packed[turn % 2].reshape(wide.shape).astype(F32)
            turn += 1
            held = src.at[parts.index(part)]
            x, z = ((ix + distance) & 3, iz) if part == 0 else (ix, (iz + distance) & 3)
            target = (x * 4 + z) * 2 + ih
            ext[0:tiles] = held[pl.ds(slot_of(part, target), tiles)]
            after = held[slot_of(part, (target + 1) & 31)]
            ext[tiles] = jnp.where(target < 31, after, jnp.zeros_like(after))

            def step_body(k, carry, part=part, held=held, target=target):
                lane = lax.broadcasted_iota(jnp.int32, (half, 128), 1)
                found = [(slot_of(part, (target + shard[k, j]) & 31), frame[k, j]) for j in range(others)]
                for r in range(rows // half):
                    at = pl.ds(r * half, half)
                    acc = [None] * tiles

                    def add(j, values, f):
                        turned = [pltpu.roll(t, lax.rem(128 - f, 128), 1) for t in values]
                        keep = lane < 128 - f
                        for q in range(tiles):
                            picked = jnp.where(keep, turned[q], turned[(q + 1) % len(values)])
                            weight = jnp.broadcast_to(wide[pl.ds((q * steps + k) * (others + 1) + j, 1), :], (half, 128))
                            term = picked.astype(F32) * weight
                            acc[q] = term if acc[q] is None else acc[q] + term

                    add(0, [ext[q, at, :] for q in range(tiles + 1)], k + 1)
                    for j, (s, at0) in enumerate(found):
                        q0 = lax.shift_right_logical(at0, 7)
                        add(j + 1, [held[s + ((q0 + q) & (tiles - 1)), at, :] for q in range(tiles)], at0 & 127)
                    for q in range(tiles):
                        mixed[pl.ds(pl.multiple_of(k * rows + r * half, half), half), q * 128 : (q + 1) * 128] = acc[q].astype(BF)
                return carry

            lax.fori_loop(0, steps, step_body, 0, unroll=4)
            term = jnp.dot(rows_of[part][...], mixed[...], preferred_element_type=F32)
            total = term if total is None else total + term
        out[...] = total.astype(BF)


def mix(jobs, shard, frame, place, pieces, rows_of, packs):
    parts = sorted({part for job in jobs for part, _ in job})
    steps, others = shard.shape
    chan, depth = rows_of[0].shape
    count, rows, _ = pieces[0][1].shape
    tiles, held = count // 4, packs[0][0].shape[0] - count
    frames = tiles * 128
    scratch = [
        pltpu.VMEM((len(parts), 8 * count, rows, 128), BF),
        pltpu.VMEM((tiles + 1, rows, 128), BF),
        pltpu.VMEM((2, held, rows, 128), BF),
        pltpu.VMEM((held * rows, 128), F32),
        pltpu.VMEM((depth, frames), BF),
        pltpu.SemaphoreType.DMA((2,)),
    ]
    ins = [shard, frame, place] + [v for part in parts for v in pieces[part]] + [rows_of[part] for part in parts]
    last = [packs[part][distance] for job in jobs for part, distance in job]
    body = functools.partial(mix_kernel, jobs, steps, others)
    specs = [SMEM] * 3 + [VMEM] * (len(ins) - 3) + [ANY] * len(last)
    return kernel_call(body, [like(chan, frames)] * len(jobs), ins + last, specs, scratch, limit=16, cost=4.0 * len(last))


def forward_kernel(n, span, last, received, x, *refs):
    stacks, outs, (by_late, by_x, by_hidden, sems) = refs[:3], list(refs[3:-4]), refs[-4:]
    copies = fetched(n, stacks, (by_late, by_x, by_hidden), sems)
    chan, frames = x.shape
    late = received
    if span < frames:
        late = outs.pop(0)
        late[:, :span] = received[...]
        late[:, span:] = x[:, : frames - span]
    hidden, slope_f, slope_g = outs[:3]
    for copy in copies:
        copy.wait()
    filt = jnp.tanh(dot(by_late[:, :chan], late[...], 0, 0) + dot(by_x[:, :chan], x[...], 0, 0))
    pre = dot(by_late[:, chan:], late[...], 0, 0) + dot(by_x[:, chan:], x[...], 0, 0)
    gate = 0.5 * jnp.tanh(0.5 * pre) + 0.5
    out = filt * gate
    hidden[...] = out.astype(BF)
    slope_f[...] = (gate * (1.0 - filt * filt)).astype(BF)
    slope_g[...] = (out * (1.0 - gate)).astype(BF)
    if not last:
        outs[3][...] = (x[...].astype(F32) + dot(by_hidden[...], hidden[...], 0, 0)).astype(BF)


def forward(n, last, span, received, x, by_late, by_x, by_hidden):
    count = (span < x.shape[1]) + 3 + (not last)
    outs = kernel_call(
        functools.partial(forward_kernel, n, span, last),
        [like(*x.shape)] * count,
        [received, x, by_late, by_x, by_hidden],
        [VMEM, VMEM] + [ANY] * 3,
        held_for(by_late, by_x, by_hidden),
        limit=12,
    )
    return outs if span < x.shape[1] else [received] + list(outs)


def first_kernel(n, count, *refs):
    terms, (slope_f, slope_g), stacks = refs[:count], refs[count : count + 2], refs[count + 2 : count + 4]
    grad, dpre, sent, by_hidden, by_late, sems = refs[count + 4 :]
    copies = fetched(n, stacks, (by_hidden, by_late), sems)
    chan = grad.shape[0]
    total = terms[0][...].astype(F32)
    for term in terms[1:]:
        total = total + term[...].astype(F32)
    grad[...] = total.astype(BF)
    copies[0].wait()
    dhid = jnp.dot(by_hidden[...], grad[...], preferred_element_type=F32)
    dpre[:chan] = (dhid * slope_f[...].astype(F32)).astype(BF)
    dpre[chan:] = (dhid * slope_g[...].astype(F32)).astype(BF)
    copies[1].wait()
    sent[...] = jnp.dot(by_late[...], dpre[...], preferred_element_type=F32).astype(BF)


def first(n, terms, by_hidden, by_late, slope_f, slope_g):
    chan, frames = slope_f.shape
    outs = [like(m, frames) for m in (chan, 2 * chan, chan)]
    ins = list(terms) + [slope_f, slope_g, by_hidden, by_late]
    specs = [VMEM] * (len(ins) - 2) + [ANY] * 2
    return kernel_call(functools.partial(first_kernel, n, len(terms)), outs, ins, specs, held_for(by_hidden, by_late))


def columns_kernel(away, place, grad, dpre, late, x, hidden, out):
    chan = x.shape[0]
    at = 1 - place[3] if away else place[3]
    rows = dpre[pl.ds(pl.multiple_of(at * chan, chan), chan), :]
    out[:, :chan] = dot(late[...], rows, 1, 1).astype(BF)
    out[:, chan : 2 * chan] = dot(x[...], rows, 1, 1).astype(BF)
    rows = grad[pl.ds(pl.multiple_of(at * (chan // 2), chan // 2), chan // 2), :]
    out[:, 2 * chan :] = dot(hidden[...], rows, 1, 1).astype(BF)


def rest_kernel(n, place, grad, dpre, late, x, hidden, stack, part, mine, by_x, sems):
    copies = fetched(n, (stack,), (by_x,), sems)
    columns_kernel(False, place, grad, dpre, late, x, hidden, mine)
    copies[0].wait()
    part[...] = grad[...].astype(F32) + jnp.dot(by_x[...], dpre[...], preferred_element_type=F32)


def rest(n, place, grad, dpre, late, x, hidden, by_x):
    chan, frames = x.shape
    columns = like(chan, 5 * chan // 2)
    ins = [place, grad, dpre, late, x, hidden]
    specs = [SMEM] + [VMEM] * 5
    other = kernel_call(functools.partial(columns_kernel, True), [columns], ins, specs, cost=1.3)[0]
    outs = [like(chan, frames, dtype=F32), columns]
    part, mine = kernel_call(functools.partial(rest_kernel, n), outs, ins + [by_x], specs + [ANY], held_for(by_x), cost=1.6)
    return part, mine, other


def pair_kernel(place, *refs):
    values, outs = refs[:-10], refs[-10:]
    count, rows, half = outs[0].shape
    for n in range(count):
        a, b = values[2 * n], values[2 * n + 1]

        def total(at, size, columns):
            span = pl.ds(pl.multiple_of(at, 16), size)
            return (a[span, columns].astype(F32) + b[span, columns].astype(F32)).astype(BF)

        for d in (0, 1, 3):
            outs[(0, 1, None, 2)[d]][n] = total(((place[0] + d) & 3) * rows, rows, slice(0, half))
        far = ((place[0] + 2) & 3) * rows
        for m in range(2):
            outs[3 + m][n] = total(far + m * (rows // 2), rows // 2, slice(0, half))
        size = rows // 4
        for x in range(4):
            for d in (0, 1, 3):
                outs[5 + (0, 1, None, 2)[d]][n, x] = total(x * rows + ((place[1] + d) & 3) * size, size, slice(half, 2 * half))
            outs[8 + x // 2][n, x % 2] = total(x * rows + ((place[1] + 2) & 3) * size, size, slice(half, 2 * half))


def relay_kernel(*refs):
    (up, down, from_low, from_high), outs = refs[:4], refs[4:6]
    half = from_low.shape[1]
    for n in range(up.shape[0]):
        outs[0][n, :half] = (up[n, :half].astype(F32) + from_low[n].astype(F32)).astype(BF)
        outs[0][n, half:] = up[n, half:]
        outs[1][n, :half] = down[n, :half]
        outs[1][n, half:] = (down[n, half:].astype(F32) + from_high[n].astype(F32)).astype(BF)


def relay(values, axis):
    own, up, down, first_half, second_half = values
    ins = [up, down, rotated(first_half, axis, 1), rotated(second_half, axis, -1)]
    up, down = kernel_call(relay_kernel, [like(*up.shape)] * 2, ins, cost=1.0)
    return [own, rotated(up, axis, 1), rotated(down, axis, -1)]


def pair(place, *values):
    chan, width = values[0].shape
    count, rows, half = len(values) // 2, chan // 4, width // 2
    outs = [like(count, rows, half)] * 3 + [like(count, rows // 2, half)] * 2
    outs += [like(count, 4, rows // 4, half)] * 3 + [like(count, 2, rows // 4, half)] * 2
    outs = kernel_call(pair_kernel, outs, [place, *values], [SMEM] + [VMEM] * len(values), cost=1.5)
    return relay(outs[:5], "x") + relay(outs[5:], "z")


def exchanged(values, first_axis, second_axis):
    return [
        v if n % 4 == 0 else rotated(v, (first_axis, second_axis)[n // 4], n % 4) for n, v in enumerate(values)
    ]


def middle_kernel(place, *refs):
    groups, outs = [refs[n : n + 6] for n in range(0, len(refs) - 8, 6)], refs[-8:]
    size = outs[0].shape[1]
    at = 0
    for group in groups:
        for n in range(group[0].shape[0]):
            for d in range(4):
                rows = pl.ds(pl.multiple_of(((place[1] + d) & 3) * size, size), size)
                total = group[0][n, rows, :].astype(F32)
                for m in range(1, 3):
                    total = total + group[m][n, rows, :].astype(F32)
                outs[d][at] = total.astype(BF)
                x = (place[0] + d) & 3
                total = group[3][n, x].astype(F32)
                for m in range(4, 6):
                    total = total + group[m][n, x].astype(F32)
                outs[4 + d][at] = total.astype(BF)
            at += 1


def middle(place, *groups):
    layers = sum(group[0].shape[0] for group in groups)
    _, rows, half = groups[0][0].shape
    ins = [place] + [v for group in groups for v in group]
    outs = kernel_call(middle_kernel, [like(layers, rows // 4, half)] * 8, ins, [SMEM] + [VMEM] * (len(ins) - 1))
    return exchanged(outs, "z", "x")


def late_kernel(place, *refs):
    parts, (keep, away) = refs[:8], refs[8:]
    rows, half = keep.shape[1], parts[0].shape[2]
    for out, h in ((away, 1 - place[2]), (keep, place[2])):
        span = pl.ds(pl.multiple_of(h * rows, rows), rows)
        for side in range(2):
            total = parts[4 * side][:, span, :].astype(F32)
            for m in range(1, 4):
                total = total + parts[4 * side + m][:, span, :].astype(F32)
            out[:, :, side * half : (side + 1) * half] = total.astype(BF)


def streams_kernel(keep, over_h, over_l, over_both, out):
    near = keep[...].astype(F32) + over_h[...].astype(F32)
    out[...] = near + (over_l[...].astype(F32) + over_both[...].astype(F32))


def split_kernel(place, mine, other, *outs):
    core = place[3]
    a, b = mine[...], other[...]
    low, high = jnp.where(core == 0, a, b), jnp.where(core == 0, b, a)
    at = 0
    for out in outs:
        size = out.shape[2] // 2
        out[:, :, :size] = low[:, :, at : at + size]
        out[:, :, size:] = high[:, :, at : at + size]
        at += size


def final_kernel(span, part, sent, received, out):
    chan, frames = part.shape
    total = (part[:, : frames - span] + sent[:, span:].astype(F32)).astype(BF)
    out[0, : frames - span] = total.T
    total = (part[:, frames - span :] + received[...].astype(F32)).astype(BF)
    out[0, frames - span :] = total.T


def on_device(features, dilated_weight, current_weight, residual_weight, predict, logit_grads, neg_shard, neg_frame):
    _, frames, chan = features.shape
    layers = dilated_weight.shape[0]
    steps, others = neg_shard.shape
    rows = chan // 8
    place = jnp.stack([lax.axis_index(a) for a in ("x", "z", "h", "c")])

    turned, blocks_a, blocks_b = prepare(place, features)
    rows_of = kernel_call(
        predict_kernel,
        [like(chan, steps * rows)] * 2,
        [place, predict],
        [SMEM, ANY],
        [pltpu.VMEM((2, steps * rows, chan), BF), pltpu.SemaphoreType.DMA((2, steps))],
        cost=4.0,
    )
    blocks_a = blocks_a[:1] + [rotated(blocks_a[d], "x", d) for d in (1, 2, 3)]
    blocks_b = blocks_b[:1] + [rotated(blocks_b[d], "z", d) for d in (1, 2, 3)]
    blocks_a, rows_of = lax.optimization_barrier((blocks_a, rows_of))
    pack_a, pack_b, sole_a, sole_b = pack(blocks_a, blocks_b, logit_grads)
    sole_a, sole_b = rotated(sole_a, "h", 1), rotated(sole_b, "h", 1)
    packs_a = [pack_a] + [rotated(pack_a, "z", -d) for d in (1, 2, 3)]
    packs_b = [pack_b] + [rotated(pack_b, "x", -d) for d in (1, 2, 3)]
    soles_a = [sole_a] + [rotated(sole_a, "z", -d) for d in (1, 2, 3)]
    soles_b = [sole_b] + [rotated(sole_b, "x", -d) for d in (1, 2, 3)]
    pieces = [[v for both in zip(*part) for v in both] for part in ((packs_a, soles_a), (packs_b, soles_b))]
    packs = [packs_b, packs_a]

    spans = [(64, 1), (512, 1), (512, 4)]
    x = turned
    saved = []
    for n in range(layers):
        span, hops = spans[n]
        if n == 1:
            x = lax.optimization_barrier((x, sole_a))[0]
        received = shifted(x[:, frames - span :], hops)
        late, hidden, slope_f, slope_g, *after = forward(
            n, n + 1 == layers, span, received, x, dilated_weight, current_weight, residual_weight
        )
        saved.append([x, late, hidden, slope_f, slope_g])
        x = after[0] if after else None

    def mixed(jobs):
        return mix(jobs, neg_shard, neg_frame, place, pieces, rows_of, packs)

    near = mixed([[(0, d)] for d in (2, 1, 3)])
    terms = [rotated(v, "x", d) for v, d in zip(near, (2, 1, 3))]
    pieces[1][0], saved[1][2], _ = lax.optimization_barrier((pieces[1][0], saved[1][2], near[0]))
    near = mixed([[(1, d)] for d in (2, 1)])
    terms += [rotated(v, "z", d) for v, d in zip(near, (2, 1))]
    terms.append(rotated(mixed([[(1, 3)]])[0], "z", 3))
    terms.append(mixed([[(0, 0), (1, 0)]])[0])

    halves = [None] * layers
    for n in reversed(range(layers)):
        x, late, hidden, slope_f, slope_g = saved[n]
        span, hops = spans[n]
        grad, dpre, sent = first(n, terms, residual_weight, dilated_weight, slope_f, slope_g)
        received = shifted(sent[:, :span], -hops)
        part, mine, other = rest(n, place, grad, dpre, late, x, hidden, current_weight)
        if n > 0:
            received, other = lax.optimization_barrier((received, other))
        halves[n] = (mine, rotated(other, "c", 1))
        terms = [part, received]
    sums = middle(place, pair(place, *halves[0], *halves[1], *halves[2]))
    keep, away = kernel_call(late_kernel, [like(layers, 16, 5 * chan // 2)] * 2, [place, *sums], [SMEM] + [VMEM] * 8)
    over_both = lax.ppermute(away, ("h", "l"), [(0, 3), (1, 2), (2, 1), (3, 0)])
    ins = [keep, rotated(away, "h", 1), rotated(keep, "l", 1), over_both]
    share = kernel_call(streams_kernel, [like(*keep.shape, dtype=F32)], ins)[0]
    input_grad = kernel_call(functools.partial(final_kernel, span), [like(1, frames, chan)], [part, sent, received])[0]
    outs = [like(layers, 16, n, dtype=F32) for n in (2 * chan, 2 * chan, chan)]
    grads = kernel_call(split_kernel, outs, [place, share, rotated(share, "c", 1)], [SMEM, VMEM, VMEM])
    return (input_grad, *grads)


def solution(mesh):
    fine = Mesh(mesh.devices.reshape(4, 4, 2, 2, 2), ("x", "z", "h", "l", "c"))
    stream = ("l", "c")
    return jax.shard_map(
        on_device,
        mesh=fine,
        in_specs=(P(stream, SEQ, None), P(), P(), P(), P(), P(stream, None, None, SEQ), P(), P()),
        out_specs=(P(stream, SEQ, None), P(None, SEQ, None), P(None, SEQ, None), P(None, SEQ, None)),
        check_vma=False,
    )
```

```python
import functools

import jax
import jax.numpy as jnp
from jax import lax
from jax.experimental import pallas as pl
from jax.experimental.pallas import tpu as pltpu
from jax.sharding import Mesh, PartitionSpec as P

SEQ = ("x", "z", "h")
BF = jnp.bfloat16
F32 = jnp.float32
VMEM = pl.BlockSpec(memory_space=pltpu.VMEM)
SMEM = pl.BlockSpec(memory_space=pltpu.SMEM)
ANY = pl.BlockSpec(memory_space=pl.ANY)
PACE = 2e9


def rotated(value, axis, steps):
    count = lax.axis_size(axis)
    return lax.ppermute(value, axis, [(i, (i + steps) % count) for i in range(count)])


def shifted(value, steps):
    count = 32
    lead, last = (max(0, -steps), min(count, count - steps))
    return lax.ppermute(value, SEQ, [(i, i + steps) for i in range(lead, last)])


def dot(a, b, ca, cb):
    return lax.dot_general(a, b, (((ca,), (cb,)), ((), ())), preferred_element_type=F32)


def like(*shape, dtype=BF):
    return jax.ShapeDtypeStruct(shape, dtype)


def held_for(*weights):
    return [pltpu.VMEM(w.shape[1:], w.dtype) for w in weights] + [pltpu.SemaphoreType.DMA((len(weights),))]


def fetched(n, stacks, held, sems):
    copies = [pltpu.make_async_copy(w.at[n], h, sems.at[m]) for m, (w, h) in enumerate(zip(stacks, held))]
    for copy in copies:
        copy.start()
    return copies


def kernel_call(body, outs, ins, specs=None, scratch=(), limit=12, cost=2.0):
    return pl.pallas_call(
        body,
        out_shape=outs,
        in_specs=specs or [VMEM] * len(ins),
        out_specs=[VMEM] * len(outs),
        scratch_shapes=list(scratch),
        compiler_params=pltpu.CompilerParams(vmem_limit_bytes=limit * 2**20),
        cost_estimate=pl.CostEstimate(flops=int(cost * PACE) + 1, bytes_accessed=1, transcendentals=0),
    )(*ins)


def prepare_kernel(place, features, turned, *blocks):
    frames, rows = turned.shape[1], blocks[0].shape[1]
    for q in range(frames // 128):
        turned[:, q * 128 : (q + 1) * 128] = features[0, q * 128 : (q + 1) * 128, :].T
    for n, block in enumerate(blocks):
        at = pl.multiple_of((n // 4 * 4 + ((place[n // 4] + n % 4) & 3)) * rows, rows)
        for q in range(frames // 128):
            block[q] = turned[pl.ds(at, rows), q * 128 : (q + 1) * 128]


def prepare(place, features):
    _, frames, chan = features.shape
    outs = [like(chan, frames)] + [like(frames // 128, chan // 8, 128)] * 8
    turned, *blocks = kernel_call(prepare_kernel, outs, [place, features], [SMEM, VMEM])
    return turned, blocks[:4], blocks[4:]


def pack_kernel(*refs):
    blocks, logits, outs, wide = (refs[:4], refs[4:8]), refs[8], refs[9:-1], refs[-1]
    steps, width = logits.shape[1:3]
    tiles, rows, _ = blocks[0][0].shape
    for q in range(tiles):
        for k in range(steps):
            at = (q * steps + k) * width
            wide[at : at + width] = logits[0, k, :, q * 128 : (q + 1) * 128]
    for part in range(2):
        pack, sole = outs[part], outs[2 + part]
        for n, block in enumerate(blocks[part]):
            pack[n * tiles : (n + 1) * tiles] = block[...]
            sole[n * tiles : (n + 1) * tiles] = block[...]
        pack[4 * tiles :] = wide[...].astype(BF).reshape(-1, rows, 128)


def pack(blocks_a, blocks_b, logits):
    tiles, rows, _ = blocks_a[0].shape
    held = -(-logits.size // 128 // rows)
    outs = [like(4 * tiles + held, rows, 128)] * 2 + [like(4 * tiles, rows, 128)] * 2
    scratch = [pltpu.VMEM((held * rows, 128), F32)]
    return kernel_call(pack_kernel, outs, [*blocks_a, *blocks_b, logits], scratch=scratch, cost=1.0)


def predict_kernel(place, predict, out_a, out_b, rows, sems):
    steps = sems.shape[1]
    chan = predict.shape[1]
    size = rows.shape[1] // steps
    copies = []
    for part, at in enumerate((place[0], 4 + place[1])):
        for k in range(steps):
            copies.append(
                pltpu.make_async_copy(
                    predict.at[pl.ds(pl.multiple_of(k * chan + at * size, size), size), :],
                    rows.at[part, pl.ds(k * size, size), :],
                    sems.at[part, k],
                )
            )
    for copy in copies:
        copy.start()
    for copy in copies:
        copy.wait()
    out_a[...] = rows[0].T
    out_b[...] = rows[1].T


def mix_kernel(jobs, steps, others, shard, frame, place, *refs):
    parts = sorted({part for job in jobs for part, _ in job})
    order = [pair for job in jobs for pair in job]
    refs = list(refs)
    pieces = {part: [refs.pop(0) for _ in range(8)] for part in parts}
    rows_of = {part: refs.pop(0) for part in parts}
    packs = [refs.pop(0) for _ in order]
    outs = [refs.pop(0) for _ in jobs]
    src, ext, packed, wide, mixed, sems = refs
    count, rows, _ = pieces[parts[0]][1].shape
    tiles = count // 4
    half = rows
    ix, iz, ih = place[0], place[1], place[2]

    def fetch(n):
        size = packed.shape[1]
        return pltpu.make_async_copy(packs[n].at[pl.ds(count, size)], packed.at[n % 2], sems.at[n % 2])

    fetch(0).start()
    for at, part in enumerate(parts):
        for n, piece in enumerate(pieces[part]):
            src[at, n * count : (n + 1) * count] = piece[:count]

    def slot_of(part, index):
        x, z = index >> 3, (index >> 1) & 3
        far, near = (z - iz, ix - x) if part == 0 else (x - ix, iz - z)
        return (((far & 3) * 2 + ((index - ih) & 1)) * 4 + (near & 3)) * tiles

    turn = 0
    for job, out in zip(jobs, outs):
        total = None
        for part, distance in job:
            fetch(turn).wait()
            if turn + 1 < len(order):
                fetch(turn + 1).start()
            wide[...] = packed[turn % 2].reshape(wide.shape).astype(F32)
            turn += 1
            held = src.at[parts.index(part)]
            x, z = ((ix + distance) & 3, iz) if part == 0 else (ix, (iz + distance) & 3)
            target = (x * 4 + z) * 2 + ih
            ext[0:tiles] = held[pl.ds(slot_of(part, target), tiles)]
            after = held[slot_of(part, (target + 1) & 31)]
            ext[tiles] = jnp.where(target < 31, after, jnp.zeros_like(after))

            def step_body(k, carry, part=part, held=held, target=target):
                lane = lax.broadcasted_iota(jnp.int32, (half, 128), 1)
                found = [(slot_of(part, (target + shard[k, j]) & 31), frame[k, j]) for j in range(others)]
                for r in range(rows // half):
                    at = pl.ds(r * half, half)
                    acc = [None] * tiles

                    def add(j, values, f):
                        turned = [pltpu.roll(t, lax.rem(128 - f, 128), 1) for t in values]
                        keep = lane < 128 - f
                        for q in range(tiles):
                            picked = jnp.where(keep, turned[q], turned[(q + 1) % len(values)])
                            weight = jnp.broadcast_to(wide[pl.ds((q * steps + k) * (others + 1) + j, 1), :], (half, 128))
                            term = picked.astype(F32) * weight
                            acc[q] = term if acc[q] is None else acc[q] + term

                    add(0, [ext[q, at, :] for q in range(tiles + 1)], k + 1)
                    for j, (s, at0) in enumerate(found):
                        q0 = lax.shift_right_logical(at0, 7)
                        add(j + 1, [held[s + ((q0 + q) & (tiles - 1)), at, :] for q in range(tiles)], at0 & 127)
                    for q in range(tiles):
                        mixed[pl.ds(pl.multiple_of(k * rows + r * half, half), half), q * 128 : (q + 1) * 128] = acc[q].astype(BF)
                return carry

            lax.fori_loop(0, steps, step_body, 0, unroll=6)
            term = jnp.dot(rows_of[part][...], mixed[...], preferred_element_type=F32)
            total = term if total is None else total + term
        out[...] = total.astype(BF)


def mix(jobs, shard, frame, place, pieces, rows_of, packs):
    parts = sorted({part for job in jobs for part, _ in job})
    steps, others = shard.shape
    chan, depth = rows_of[0].shape
    count, rows, _ = pieces[0][1].shape
    tiles, held = count // 4, packs[0][0].shape[0] - count
    frames = tiles * 128
    scratch = [
        pltpu.VMEM((len(parts), 8 * count, rows, 128), BF),
        pltpu.VMEM((tiles + 1, rows, 128), BF),
        pltpu.VMEM((2, held, rows, 128), BF),
        pltpu.VMEM((held * rows, 128), F32),
        pltpu.VMEM((depth, frames), BF),
        pltpu.SemaphoreType.DMA((2,)),
    ]
    ins = [shard, frame, place] + [v for part in parts for v in pieces[part]] + [rows_of[part] for part in parts]
    last = [packs[part][distance] for job in jobs for part, distance in job]
    body = functools.partial(mix_kernel, jobs, steps, others)
    specs = [SMEM] * 3 + [VMEM] * (len(ins) - 3) + [ANY] * len(last)
    return kernel_call(body, [like(chan, frames)] * len(jobs), ins + last, specs, scratch, limit=16, cost=4.0 * len(last))


def forward_kernel(n, span, last, received, x, *refs):
    stacks, outs, (by_late, by_x, by_hidden, sems) = refs[:3], list(refs[3:-4]), refs[-4:]
    copies = fetched(n, stacks, (by_late, by_x, by_hidden), sems)
    chan, frames = x.shape
    late = received
    if span < frames:
        late = outs.pop(0)
        late[:, :span] = received[...]
        late[:, span:] = x[:, : frames - span]
    hidden, slope_f, slope_g = outs[:3]
    for copy in copies:
        copy.wait()
    filt = jnp.tanh(dot(by_late[:, :chan], late[...], 0, 0) + dot(by_x[:, :chan], x[...], 0, 0))
    pre = dot(by_late[:, chan:], late[...], 0, 0) + dot(by_x[:, chan:], x[...], 0, 0)
    gate = 0.5 * jnp.tanh(0.5 * pre) + 0.5
    out = filt * gate
    hidden[...] = out.astype(BF)
    slope_f[...] = (gate * (1.0 - filt * filt)).astype(BF)
    slope_g[...] = (out * (1.0 - gate)).astype(BF)
    if not last:
        outs[3][...] = (x[...].astype(F32) + dot(by_hidden[...], hidden[...], 0, 0)).astype(BF)


def forward(n, last, span, received, x, by_late, by_x, by_hidden):
    count = (span < x.shape[1]) + 3 + (not last)
    outs = kernel_call(
        functools.partial(forward_kernel, n, span, last),
        [like(*x.shape)] * count,
        [received, x, by_late, by_x, by_hidden],
        [VMEM, VMEM] + [ANY] * 3,
        held_for(by_late, by_x, by_hidden),
        limit=12,
    )
    return outs if span < x.shape[1] else [received] + list(outs)


def first_kernel(n, count, *refs):
    terms, (slope_f, slope_g), stacks = refs[:count], refs[count : count + 2], refs[count + 2 : count + 4]
    grad, dpre, sent, by_hidden, by_late, sems = refs[count + 4 :]
    copies = fetched(n, stacks, (by_hidden, by_late), sems)
    chan = grad.shape[0]
    total = terms[0][...].astype(F32)
    for term in terms[1:]:
        total = total + term[...].astype(F32)
    grad[...] = total.astype(BF)
    copies[0].wait()
    dhid = jnp.dot(by_hidden[...], grad[...], preferred_element_type=F32)
    dpre[:chan] = (dhid * slope_f[...].astype(F32)).astype(BF)
    dpre[chan:] = (dhid * slope_g[...].astype(F32)).astype(BF)
    copies[1].wait()
    sent[...] = jnp.dot(by_late[...], dpre[...], preferred_element_type=F32).astype(BF)


def first(n, terms, by_hidden, by_late, slope_f, slope_g):
    chan, frames = slope_f.shape
    outs = [like(m, frames) for m in (chan, 2 * chan, chan)]
    ins = list(terms) + [slope_f, slope_g, by_hidden, by_late]
    specs = [VMEM] * (len(ins) - 2) + [ANY] * 2
    return kernel_call(functools.partial(first_kernel, n, len(terms)), outs, ins, specs, held_for(by_hidden, by_late))


def columns_kernel(away, place, grad, dpre, late, x, hidden, out):
    chan = x.shape[0]
    at = 1 - place[3] if away else place[3]
    rows = dpre[pl.ds(pl.multiple_of(at * chan, chan), chan), :]
    out[:, :chan] = dot(late[...], rows, 1, 1).astype(BF)
    out[:, chan : 2 * chan] = dot(x[...], rows, 1, 1).astype(BF)
    rows = grad[pl.ds(pl.multiple_of(at * (chan // 2), chan // 2), chan // 2), :]
    out[:, 2 * chan :] = dot(hidden[...], rows, 1, 1).astype(BF)


def rest_kernel(n, place, grad, dpre, late, x, hidden, stack, part, mine, by_x, sems):
    copies = fetched(n, (stack,), (by_x,), sems)
    columns_kernel(False, place, grad, dpre, late, x, hidden, mine)
    copies[0].wait()
    part[...] = grad[...].astype(F32) + jnp.dot(by_x[...], dpre[...], preferred_element_type=F32)


def rest(n, place, grad, dpre, late, x, hidden, by_x):
    chan, frames = x.shape
    columns = like(chan, 5 * chan // 2)
    ins = [place, grad, dpre, late, x, hidden]
    specs = [SMEM] + [VMEM] * 5
    other = kernel_call(functools.partial(columns_kernel, True), [columns], ins, specs, cost=1.3)[0]
    outs = [like(chan, frames, dtype=F32), columns]
    part, mine = kernel_call(functools.partial(rest_kernel, n), outs, ins + [by_x], specs + [ANY], held_for(by_x), cost=1.6)
    return part, mine, other


def pair_kernel(place, *refs):
    values, outs = refs[:-10], refs[-10:]
    count, rows, half = outs[0].shape
    for n in range(count):
        a, b = values[2 * n], values[2 * n + 1]

        def total(at, size, columns):
            span = pl.ds(pl.multiple_of(at, 16), size)
            return (a[span, columns].astype(F32) + b[span, columns].astype(F32)).astype(BF)

        for d in (0, 1, 3):
            outs[(0, 1, None, 2)[d]][n] = total(((place[0] + d) & 3) * rows, rows, slice(0, half))
        far = ((place[0] + 2) & 3) * rows
        for m in range(2):
            outs[3 + m][n] = total(far + m * (rows // 2), rows // 2, slice(0, half))
        size = rows // 4
        for x in range(4):
            for d in (0, 1, 3):
                outs[5 + (0, 1, None, 2)[d]][n, x] = total(x * rows + ((place[1] + d) & 3) * size, size, slice(half, 2 * half))
            outs[8 + x // 2][n, x % 2] = total(x * rows + ((place[1] + 2) & 3) * size, size, slice(half, 2 * half))


def relay_kernel(*refs):
    (up, down, from_low, from_high), outs = refs[:4], refs[4:6]
    half = from_low.shape[1]
    for n in range(up.shape[0]):
        outs[0][n, :half] = (up[n, :half].astype(F32) + from_low[n].astype(F32)).astype(BF)
        outs[0][n, half:] = up[n, half:]
        outs[1][n, :half] = down[n, :half]
        outs[1][n, half:] = (down[n, half:].astype(F32) + from_high[n].astype(F32)).astype(BF)


def relay(values, axis):
    own, up, down, first_half, second_half = values
    ins = [up, down, rotated(first_half, axis, 1), rotated(second_half, axis, -1)]
    up, down = kernel_call(relay_kernel, [like(*up.shape)] * 2, ins, cost=1.0)
    return [own, rotated(up, axis, 1), rotated(down, axis, -1)]


def pair(place, *values):
    chan, width = values[0].shape
    count, rows, half = len(values) // 2, chan // 4, width // 2
    outs = [like(count, rows, half)] * 3 + [like(count, rows // 2, half)] * 2
    outs += [like(count, 4, rows // 4, half)] * 3 + [like(count, 2, rows // 4, half)] * 2
    outs = kernel_call(pair_kernel, outs, [place, *values], [SMEM] + [VMEM] * len(values), cost=1.5)
    return relay(outs[:5], "x") + relay(outs[5:], "z")


def exchanged(values, first_axis, second_axis):
    return [
        v if n % 4 == 0 else rotated(v, (first_axis, second_axis)[n // 4], n % 4) for n, v in enumerate(values)
    ]


def middle_kernel(place, *refs):
    groups, outs = [refs[n : n + 6] for n in range(0, len(refs) - 8, 6)], refs[-8:]
    size = outs[0].shape[1]
    at = 0
    for group in groups:
        for n in range(group[0].shape[0]):
            for d in range(4):
                rows = pl.ds(pl.multiple_of(((place[1] + d) & 3) * size, size), size)
                total = group[0][n, rows, :].astype(F32)
                for m in range(1, 3):
                    total = total + group[m][n, rows, :].astype(F32)
                outs[d][at] = total.astype(BF)
                x = (place[0] + d) & 3
                total = group[3][n, x].astype(F32)
                for m in range(4, 6):
                    total = total + group[m][n, x].astype(F32)
                outs[4 + d][at] = total.astype(BF)
            at += 1


def middle(place, *groups):
    layers = sum(group[0].shape[0] for group in groups)
    _, rows, half = groups[0][0].shape
    ins = [place] + [v for group in groups for v in group]
    outs = kernel_call(middle_kernel, [like(layers, rows // 4, half)] * 8, ins, [SMEM] + [VMEM] * (len(ins) - 1))
    return exchanged(outs, "z", "x")


def late_kernel(place, *refs):
    parts, (keep, away) = refs[:8], refs[8:]
    rows, half = keep.shape[1], parts[0].shape[2]
    for out, h in ((away, 1 - place[2]), (keep, place[2])):
        span = pl.ds(pl.multiple_of(h * rows, rows), rows)
        for side in range(2):
            total = parts[4 * side][:, span, :].astype(F32)
            for m in range(1, 4):
                total = total + parts[4 * side + m][:, span, :].astype(F32)
            out[:, :, side * half : (side + 1) * half] = total.astype(BF)


def streams_kernel(keep, over_h, over_l, over_both, out):
    near = keep[...].astype(F32) + over_h[...].astype(F32)
    out[...] = near + (over_l[...].astype(F32) + over_both[...].astype(F32))


def split_kernel(place, mine, other, *outs):
    core = place[3]
    a, b = mine[...], other[...]
    low, high = jnp.where(core == 0, a, b), jnp.where(core == 0, b, a)
    at = 0
    for out in outs:
        size = out.shape[2] // 2
        out[:, :, :size] = low[:, :, at : at + size]
        out[:, :, size:] = high[:, :, at : at + size]
        at += size


def final_kernel(span, part, sent, received, out):
    chan, frames = part.shape
    total = (part[:, : frames - span] + sent[:, span:].astype(F32)).astype(BF)
    out[0, : frames - span] = total.T
    total = (part[:, frames - span :] + received[...].astype(F32)).astype(BF)
    out[0, frames - span :] = total.T


def on_device(features, dilated_weight, current_weight, residual_weight, predict, logit_grads, neg_shard, neg_frame):
    _, frames, chan = features.shape
    layers = dilated_weight.shape[0]
    steps, others = neg_shard.shape
    rows = chan // 8
    place = jnp.stack([lax.axis_index(a) for a in ("x", "z", "h", "c")])

    turned, blocks_a, blocks_b = prepare(place, features)
    rows_of = kernel_call(
        predict_kernel,
        [like(chan, steps * rows)] * 2,
        [place, predict],
        [SMEM, ANY],
        [pltpu.VMEM((2, steps * rows, chan), BF), pltpu.SemaphoreType.DMA((2, steps))],
        cost=4.0,
    )
    blocks_a = blocks_a[:1] + [rotated(blocks_a[d], "x", d) for d in (1, 2, 3)]
    blocks_b = blocks_b[:1] + [rotated(blocks_b[d], "z", d) for d in (1, 2, 3)]
    blocks_a, rows_of = lax.optimization_barrier((blocks_a, rows_of))
    pack_a, pack_b, sole_a, sole_b = pack(blocks_a, blocks_b, logit_grads)
    sole_a, sole_b = rotated(sole_a, "h", 1), rotated(sole_b, "h", 1)
    packs_a = [pack_a] + [rotated(pack_a, "z", -d) for d in (1, 2, 3)]
    packs_b = [pack_b] + [rotated(pack_b, "x", -d) for d in (1, 2, 3)]
    soles_a = [sole_a] + [rotated(sole_a, "z", -d) for d in (1, 2, 3)]
    soles_b = [sole_b] + [rotated(sole_b, "x", -d) for d in (1, 2, 3)]
    pieces = [[v for both in zip(*part) for v in both] for part in ((packs_a, soles_a), (packs_b, soles_b))]
    packs = [packs_b, packs_a]

    spans = [(64, 1), (512, 1), (512, 4)]
    x = turned
    saved = []
    for n in range(layers):
        span, hops = spans[n]
        if n == 1:
            x = lax.optimization_barrier((x, sole_a))[0]
        received = shifted(x[:, frames - span :], hops)
        late, hidden, slope_f, slope_g, *after = forward(
            n, n + 1 == layers, span, received, x, dilated_weight, current_weight, residual_weight
        )
        saved.append([x, late, hidden, slope_f, slope_g])
        x = after[0] if after else None

    def mixed(jobs):
        return mix(jobs, neg_shard, neg_frame, place, pieces, rows_of, packs)

    near = mixed([[(0, d)] for d in (2, 1, 3)])
    terms = [rotated(v, "x", d) for v, d in zip(near, (2, 1, 3))]
    pieces[1][0], saved[1][2], _ = lax.optimization_barrier((pieces[1][0], saved[1][2], near[0]))
    near = mixed([[(1, d)] for d in (2, 1)])
    terms += [rotated(v, "z", d) for v, d in zip(near, (2, 1))]
    terms.append(rotated(mixed([[(1, 3)]])[0], "z", 3))
    terms.append(mixed([[(0, 0), (1, 0)]])[0])

    halves = [None] * layers
    for n in reversed(range(layers)):
        x, late, hidden, slope_f, slope_g = saved[n]
        span, hops = spans[n]
        grad, dpre, sent = first(n, terms, residual_weight, dilated_weight, slope_f, slope_g)
        received = shifted(sent[:, :span], -hops)
        part, mine, other = rest(n, place, grad, dpre, late, x, hidden, current_weight)
        if n > 0:
            received, other = lax.optimization_barrier((received, other))
        halves[n] = (mine, rotated(other, "c", 1))
        terms = [part, received]
    sums = middle(place, pair(place, *halves[0], *halves[1], *halves[2]))
    keep, away = kernel_call(late_kernel, [like(layers, 16, 5 * chan // 2)] * 2, [place, *sums], [SMEM] + [VMEM] * 8)
    over_both = lax.ppermute(away, ("h", "l"), [(0, 3), (1, 2), (2, 1), (3, 0)])
    ins = [keep, rotated(away, "h", 1), rotated(keep, "l", 1), over_both]
    share = kernel_call(streams_kernel, [like(*keep.shape, dtype=F32)], ins)[0]
    input_grad = kernel_call(functools.partial(final_kernel, span), [like(1, frames, chan)], [part, sent, received])[0]
    outs = [like(layers, 16, n, dtype=F32) for n in (2 * chan, 2 * chan, chan)]
    grads = kernel_call(split_kernel, outs, [place, share, rotated(share, "c", 1)], [SMEM, VMEM, VMEM])
    return (input_grad, *grads)


def solution(mesh):
    fine = Mesh(mesh.devices.reshape(4, 4, 2, 2, 2), ("x", "z", "h", "l", "c"))
    stream = ("l", "c")
    return jax.shard_map(
        on_device,
        mesh=fine,
        in_specs=(P(stream, SEQ, None), P(), P(), P(), P(), P(stream, None, None, SEQ), P(), P()),
        out_specs=(P(stream, SEQ, None), P(None, SEQ, None), P(None, SEQ, None), P(None, SEQ, None)),
        check_vma=False,
    )
```
